256 devices in a mesh: patch: 64 (over y_hi, x, z), head: 4 (over y_lo, core).
Axes of the slice: x: 4, y: 4 (y_hi: 2, y_lo: 2; y = y_hi * 2 + y_lo), z: 8, core: 2. Of those that a mesh axis runs over, the one named last changes fastest.
Arguments:
- image_hidden: bfloat16 [2, 4096, 3072], P(None, 'patch', 'head'), may hold values from -6 to 6
- text_kv: bfloat16 [2, 2, 512, 1536], P(None, None, 'patch', 'head'), may hold values from -96 to 96
- prev_kv: bfloat16 [2, 2, 4096, 1536], P(None, None, None, 'head'), may hold values from -12 to 12
- scale_exp: int32 [2, 2, 4096, 12], P(None, None, 'patch', 'head'), may hold values from -8 to 0
- w_qkv: bfloat16 [3072, 3, 1536], P('patch', None, 'head'), may hold values from -0.109375 to 0.109375
- w_out: bfloat16 [1536, 3072], P('head', 'patch'), may hold values from -0.15625 to 0.15625
- mod_table: bfloat16 [28, 3, 3072], P(None, None, 'head'), may hold values from -4 to 4
- timesteps: int32 [2], replicated, may hold values from 0 to 27, as said below
- q_gain: float32 [128], replicated, may hold values from 1 to 1.8
- k_gain: float32 [128], replicated, may hold values from 1 to 1.8
Outputs:
- branch: bfloat16 [2, 4096, 3072], P(None, 'patch', 'head')
The draws below stay inside these ranges and needn't reach their ends.
Inputs may be any that keep to these rules, and one draw needn't show every extreme that they name: `timesteps`: the images of a batch are at distinct plan points, one of them the last.
All inputs are finite; a program needn't handle non-finite values.
Results may differ from the reference program's by a relative error of at most 0.017.
Values may be sent and summed in bfloat16 or wider, within the bound.
No kernel may reach another device: no remote copies, remote signals or barrier semaphores. Data moves between devices by JAX's collectives and lax.ppermute only.
A program may use at most 192 MiB of HBM per device.

```python
import math
import jax
import jax.numpy as jnp
from jax import lax

D = 3072
HEADS = 12
HD = 128
SCHED = 28
BATCH = 2
NIMG = 4096
TXT = 512


def draw_text_kv(key, part):
    key = jax.random.fold_in(key, 11)
    shape = (2, BATCH, TXT, HEADS * HD)
    base = jnp.clip(2.0 * jax.random.normal(key, shape, jnp.float32), -12.0, 12.0)
    return base.astype(jnp.bfloat16)


def draw_timesteps(key, part):
    key = jax.random.fold_in(key, 23)
    first, second = jax.random.split(key)
    earlier_points = jax.random.permutation(first, jnp.arange(SCHED - 1, dtype=jnp.int32))[:BATCH - 1]
    chosen = jnp.concatenate([jnp.full((1,), SCHED - 1, jnp.int32), earlier_points.astype(jnp.int32)])
    return jax.random.permutation(second, chosen).astype(jnp.int32)


def with_ends(entries, own_key, smallest, top_value):
    dims = entries.shape
    spot = [jax.random.randint(jax.random.fold_in(own_key, axis), (), 0, dims[axis]) for axis in range(len(dims))]
    entries = entries.at[tuple(spot)].set(smallest)
    longest = dims.index(max(dims))
    spot[longest] = (spot[longest] + 1) % dims[longest]
    return entries.at[tuple(spot)].set(top_value)


def steps_of(key, shape, cuts, smallest, top_value):
    level, own = 1.0, jax.random.fold_in(key, 6)
    for axis_at, parts in cuts:
        steps = jnp.exp(jax.random.uniform(jax.random.fold_in(own, axis_at), (parts,), jnp.float32, smallest / len(cuts), top_value / len(cuts)))
        level = level * jnp.repeat(steps, shape[axis_at] // parts).reshape([-1 if axis == axis_at else 1 for axis in range(len(shape))])
    return level


def bell_draw(stream_key, extent, deviation, reach, cuts=(), held_as=jnp.bfloat16):
    values = deviation * jax.random.normal(stream_key, extent, jnp.float32)
    if cuts:
        values = values * steps_of(stream_key, extent, cuts, -0.22, 0.18)
    return jnp.clip(values, -reach, reach).astype(held_as)


def setup_inputs(seed: int = 0) -> dict:
    seeds = jax.random.split(jax.random.key(seed), 11)
    image_hidden = bell_draw(seeds[0], (BATCH, NIMG, D), 1.0, 6.0, ((1, 64), (2, 4)))
    text_kv = draw_text_kv(jax.random.fold_in(seeds[10], 71), 0)
    prev_kv = bell_draw(seeds[2], (2, BATCH, NIMG, HEADS * HD), 2.0, 12.0, ((3, 4),))
    scale_exp = with_ends(jax.random.randint(seeds[3], (2, BATCH, NIMG, HEADS), -8, 1), jax.random.fold_in(seeds[3], 1), -8, 0).astype(jnp.int32)
    w_qkv = bell_draw(seeds[4], (D, 3, HEADS * HD), D ** -0.5, 0.109375, ((0, 64), (2, 4)))
    w_out = bell_draw(seeds[5], (HEADS * HD, D), (HEADS * HD) ** -0.5, 0.15625, ((0, 4), (1, 64)))
    mod_table = bell_draw(seeds[6], (SCHED, 3, D), 0.7, 4.0, ((2, 4),))
    timesteps = draw_timesteps(jax.random.fold_in(seeds[10], 71), 0)
    q_gain = jnp.clip(jnp.exp(jax.random.uniform(seeds[8], (HD,), jnp.float32, math.log(1.0), math.log(1.8))), 1.0, 1.8)
    k_gain = jnp.clip(jnp.exp(jax.random.uniform(seeds[9], (HD,), jnp.float32, math.log(1.0), math.log(1.8))), 1.0, 1.8)
    return dict(image_hidden=image_hidden, text_kv=text_kv, prev_kv=prev_kv, scale_exp=scale_exp, w_qkv=w_qkv, w_out=w_out, mod_table=mod_table, timesteps=timesteps, q_gain=q_gain, k_gain=k_gain)


EPSILON = 1e-06
CODE_LIMIT = 448.0

def finalize_output(values):
    return lax.optimization_barrier(values.astype(jnp.bfloat16)).astype(jnp.float32)

def power_two(exponents, polarity):
    summed_powers = jnp.zeros(exponents.shape, jnp.float32)
    for exponent in range(-8, 1):
        summed_powers = summed_powers + jnp.where(exponents == exponent, jnp.float32(2.0 ** (polarity * exponent)), jnp.float32(0.0))
    return summed_powers

def rms_scale(vectors, softmax_scaling):
    return vectors * lax.rsqrt(lax.optimization_barrier(jnp.mean(vectors * vectors, axis=-1, keepdims=True)) + EPSILON) * softmax_scaling

def one_head(operands):
    query_rows, image_key_rows, image_value_rows, text_key_rows, text_value_rows = operands
    softmax_scaling = HD ** (-0.5)
    image_score_logits = jnp.einsum('zoy,zny->zon', query_rows, image_key_rows) * softmax_scaling
    text_score_logits = jnp.einsum('zoy,zny->zon', query_rows, text_key_rows) * softmax_scaling
    peak = jnp.maximum(lax.optimization_barrier(jnp.max(image_score_logits, axis=-1)), lax.optimization_barrier(jnp.max(text_score_logits, axis=-1)))[..., None]
    image_exp_terms = jnp.exp(image_score_logits - peak)
    text_exp_terms = jnp.exp(text_score_logits - peak)
    denominator = lax.optimization_barrier(jnp.sum(image_exp_terms, axis=-1)) + lax.optimization_barrier(jnp.sum(text_exp_terms, axis=-1))
    weighted_values = jnp.einsum('ngo,noh->ngh', finalize_output(image_exp_terms), image_value_rows)
    weighted_values = weighted_values + jnp.einsum('ngo,noh->ngh', finalize_output(text_exp_terms), text_value_rows)
    return weighted_values / denominator[..., None]

def reference(image_hidden, text_kv, prev_kv, scale_exp, w_qkv, w_out, mod_table, timesteps, q_gain, k_gain):
    modulation = mod_table[timesteps].astype(jnp.float32)
    hidden = image_hidden.astype(jnp.float32)
    centre = lax.optimization_barrier(jnp.mean(hidden, axis=-1, keepdims=True))
    variance = lax.optimization_barrier(jnp.mean((hidden - centre) * (hidden - centre), axis=-1, keepdims=True))
    normed = finalize_output((hidden - centre) * lax.rsqrt(variance + EPSILON) * (1.0 + modulation[:, 1:2]) + modulation[:, 0:1])
    projected = jnp.einsum('brd,dce->brce', normed, w_qkv.astype(jnp.float32))
    split_shape = (BATCH, NIMG, HEADS, HD)
    queries = finalize_output(rms_scale(projected[:, :, 0].reshape(split_shape), q_gain))
    fresh_keys = rms_scale(projected[:, :, 1].reshape(split_shape), k_gain)
    fresh_values = projected[:, :, 2].reshape(split_shape)
    earlier = prev_kv.astype(jnp.float32).reshape((2,) + split_shape)
    residual = jnp.stack([fresh_keys, fresh_values]) - earlier
    block_codes = finalize_output(jnp.clip(residual * power_two(scale_exp, -1)[..., None], -CODE_LIMIT, CODE_LIMIT))
    restored = finalize_output(earlier + block_codes * power_two(scale_exp, 1)[..., None])
    text_pair = text_kv.astype(jnp.float32).reshape((2, BATCH, TXT, HEADS, HD))
    per_head = lax.map(one_head, (jnp.moveaxis(queries, 2, 0), jnp.moveaxis(restored[0], 2, 0), jnp.moveaxis(restored[1], 2, 0), jnp.moveaxis(text_pair[0], 2, 0), jnp.moveaxis(text_pair[1], 2, 0)))
    attended = finalize_output(jnp.moveaxis(per_head, 0, 2).reshape(BATCH, NIMG, HEADS * HD))
    output = jnp.einsum('brc,cd->brd', attended, w_out.astype(jnp.float32))
    return (modulation[:, 2:3] * output).astype(jnp.bfloat16)
```

```python
import jax
import jax.numpy as jnp
from jax import lax
from jax.experimental import pallas as pl
from jax.experimental.pallas import tpu as pltpu
from jax.sharding import Mesh, PartitionSpec as P

HD = 128
EPSILON = 1e-06
CODE_LIMIT = 448.0
LOG2E = 1.4426950408889634
VMEM_BYTES = 56 * 1024 * 1024

YX = ("yh", "x")
Z = ("zo", "zi")
H = ("yl", "c")


def call(kernel, out_shapes, operands, scratch=(), flops=0, moved=0):
    return pl.pallas_call(
        kernel,
        out_shape=out_shapes,
        in_specs=[pl.BlockSpec(memory_space=pltpu.VMEM)] * len(operands),
        out_specs=jax.tree.map(lambda _: pl.BlockSpec(memory_space=pltpu.VMEM), out_shapes),
        scratch_shapes=scratch,
        compiler_params=pltpu.CompilerParams(vmem_limit_bytes=VMEM_BYTES),
        cost_estimate=pl.CostEstimate(flops=flops, bytes_accessed=moved, transcendentals=0),
    )(*operands)


def norm_kernel(rows_ref, out_ref):
    features = 4 * 768
    for image in range(2):
        shift = rows_ref[:, 128 + 2 * image : 129 + 2 * image, :].astype(jnp.float32)
        scale = 1.0 + rows_ref[:, 129 + 2 * image : 130 + 2 * image, :].astype(jnp.float32)
        for start in range(0, 64, 16):
            at = image * 64 + start
            hidden = rows_ref[:, at : at + 16, :].astype(jnp.float32)
            centre = jnp.sum(jnp.sum(hidden, axis=0), axis=-1, keepdims=True) / features
            off = hidden - centre[None]
            variance = jnp.sum(jnp.sum(off * off, axis=0), axis=-1, keepdims=True) / features
            normed = (off * lax.rsqrt(variance + EPSILON)[None] * scale + shift).astype(jnp.bfloat16)
            for y in range(2):
                for x in range(4):
                    for place, block in enumerate((4 * y + x, 4 * (1 - y) + x)):
                        piece = normed[block // 2][:, (block % 2) * 384 : (block % 2) * 384 + 384]
                        out_ref[4 * y + x, at : at + 16, place * 384 : place * 384 + 384] = piece


def project_kernel(rows_ref, weights_ref, out_ref):
    weights = weights_ref[...].reshape(384, 1536)
    for x in range(4):
        rows = jnp.concatenate([rows_ref[x], rows_ref[4 + x]], axis=0)
        own, other = rows[:, :384], rows[:, 384:]
        most = jnp.dot(own, weights[:, :512], preferred_element_type=jnp.float32) + jnp.dot(
            other, weights[:, 512:1024], preferred_element_type=jnp.float32
        )
        rest = jnp.dot(own, weights[:, 1024:1152], preferred_element_type=jnp.float32)
        both = jnp.concatenate([most, rest], axis=1).astype(jnp.bfloat16)
        for image in range(2):
            for y in range(2):
                piece = both[y * 128 + image * 64 : y * 128 + image * 64 + 64]
                out_ref[4 * image + x, y * 64 : y * 64 + 64, :] = piece


def rms_scale(vectors, gain):
    return vectors * lax.rsqrt(jnp.mean(vectors * vectors, axis=-1, keepdims=True) + EPSILON) * gain


def restore_kernel(
    part_ref, prev_ref, scale_ref, text_ref, q_gain_ref, k_gain_ref, q_ref, kv_ref
):
    q_gain, k_gain = q_gain_ref[...], k_gain_ref[...]

    def total(sources, at):
        acc = part_ref[sources[0], :, at : at + HD].astype(jnp.float32)
        for source in sources[1:]:
            acc = acc + part_ref[source, :, at : at + HD].astype(jnp.float32)
        return acc

    low, high = (0, 1, 2, 3), (4, 5, 6, 7)
    key_places = ((low, 384), (low + high, 512), (high, 384))

    def restored(fresh, kind, head):
        earlier = prev_ref[kind, :, head * HD : head * HD + HD].astype(jnp.float32)
        lane = kind * 3 + head
        scale = scale_ref[:, lane : lane + 1].astype(jnp.float32)
        limit = CODE_LIMIT * scale
        scaled = jnp.clip(fresh - earlier, -limit, limit).astype(jnp.bfloat16).astype(jnp.float32)
        return (earlier + scaled).astype(jnp.bfloat16)

    for head in range(3):
        lanes = slice(head * HD, head * HD + HD)
        q_ref[:, lanes] = rms_scale(total(low, head * HD), q_gain).astype(jnp.bfloat16)
        keys = restored(rms_scale(total(*key_places[head]), k_gain), 0, head)
        values = restored(total(high, head * HD), 1, head)
        for peer in range(8):
            kv_ref[peer, 0:128, lanes] = keys
            kv_ref[peer, 144:272, lanes] = values
    for peer in range(8):
        kv_ref[peer, 128:144, :] = text_ref[0]
        kv_ref[peer, 272:288, :] = text_ref[1]


def split_three(value):
    first = value.astype(jnp.bfloat16)
    rest = value - first.astype(jnp.float32)
    second = rest.astype(jnp.bfloat16)
    third = (rest - second.astype(jnp.float32)).astype(jnp.bfloat16)
    return first, second, third


def attend_kernel(q0_ref, q1_ref, q2_ref, q3_ref, kv_ref, o0_ref, o1_ref, o2_ref, o3_ref):
    factor = LOG2E * HD**-0.5
    lane = lax.broadcasted_iota(jnp.int32, (128, HD), 1)
    stats = [jnp.zeros((128, HD), jnp.float32) for _ in range(4)]
    for head in range(3):
        lanes = slice(head * HD, head * HD + HD)
        keys = kv_ref[:, 0:144, lanes].reshape(1152, HD)
        values = kv_ref[:, 144:288, lanes].reshape(1152, HD)
        for block, (q_ref, o_ref) in enumerate(
            ((q0_ref, o0_ref), (q1_ref, o1_ref), (q2_ref, o2_ref), (q3_ref, o3_ref))
        ):
            logits = lax.dot_general(
                q_ref[:, lanes], keys, (((1,), (1,)), ((), ())), preferred_element_type=jnp.float32
            )
            peak = jnp.max(logits, axis=-1, keepdims=True)
            terms = jnp.exp2((logits - peak) * factor)
            total = jnp.sum(terms, axis=-1, keepdims=True)
            mixed = jnp.dot(terms.astype(jnp.bfloat16), values, preferred_element_type=jnp.float32)
            o_ref[:, lanes] = (mixed / total).astype(jnp.bfloat16)
            for place, part in enumerate(split_three(peak * factor + jnp.log2(total))):
                stats[block] = jnp.where(
                    lane == head * 3 + place, part.astype(jnp.float32), stats[block]
                )
    for block, o_ref in enumerate((o0_ref, o1_ref, o2_ref, o3_ref)):
        o_ref[:, 384:512] = stats[block].astype(jnp.bfloat16)


def output_kernel(p0_ref, p1_ref, p2_ref, p3_ref, weights_ref, out_ref, attended_ref):
    parts = (p0_ref, p1_ref, p2_ref, p3_ref)
    for head in range(3):
        lanes = slice(head * HD, head * HD + HD)
        sizes = []
        for ref in parts:
            stat = ref[:, 384:512].astype(jnp.float32)
            sizes.append(
                stat[:, head * 3 : head * 3 + 1]
                + stat[:, head * 3 + 1 : head * 3 + 2]
                + stat[:, head * 3 + 2 : head * 3 + 3]
            )
        top = jnp.maximum(jnp.maximum(sizes[0], sizes[1]), jnp.maximum(sizes[2], sizes[3]))
        shares = [jnp.exp2(size - top) for size in sizes]
        whole = shares[0] + shares[1] + shares[2] + shares[3]
        mixed = shares[0] * parts[0][:, lanes].astype(jnp.float32)
        for share, ref in zip(shares[1:], parts[1:]):
            mixed = mixed + share * ref[:, lanes].astype(jnp.float32)
        attended_ref[:, lanes] = (mixed / whole).astype(jnp.bfloat16)
    attended = attended_ref[...]
    for block in range(8):
        sums = lax.dot_general(
            attended,
            weights_ref[block],
            (((1,), (1,)), ((), ())),
            preferred_element_type=jnp.float32,
        ).astype(jnp.bfloat16)
        at = (block % 2) * 384
        for y in range(2):
            out_ref[4 * y + block // 2, :, at : at + 384] = sums[y * 64 : y * 64 + 64]


def gate_kernel(parts_ref, gate_ref, out_ref):
    for image in range(2):
        acc = parts_ref[4 * image].astype(jnp.float32)
        for source in range(1, 4):
            acc = acc + parts_ref[4 * image + source].astype(jnp.float32)
        gate = gate_ref[image : image + 1, :].astype(jnp.float32)
        out_ref[image] = (gate * acc).astype(jnp.bfloat16)


def power_two(exponents):
    summed = jnp.zeros(exponents.shape, jnp.float32)
    for exponent in range(-8, 1):
        summed = summed + jnp.where(exponents == exponent, jnp.float32(2.0**exponent), 0.0)
    return summed


def shape(*dims):
    return jax.ShapeDtypeStruct(dims, jnp.bfloat16)


def per_device(
    image_hidden, text_kv, prev_kv, scale_exp, w_qkv, w_out, mod_table, timesteps, q_gain, k_gain
):
    yh, x = lax.axis_index("yh"), lax.axis_index("x")
    z = lax.axis_index(Z)
    lower = yh == 0
    picked = jnp.stack(
        [lax.dynamic_index_in_dim(mod_table, timesteps[image], 0, False) for image in range(2)]
    )

    by_part = jnp.transpose(w_qkv, (1, 0, 2))
    for_low = jnp.concatenate([by_part[0], by_part[1][:, :HD]], axis=1)
    for_high = jnp.concatenate([by_part[2], by_part[1][:, 2 * HD :]], axis=1)
    kept, sent = jnp.where(lower, for_low, for_high), jnp.where(lower, for_high, for_low)
    scales = jnp.transpose(power_two(scale_exp), (1, 2, 0, 3)).reshape(2, 64, 6).astype(jnp.bfloat16)
    scales = jnp.pad(scales, ((0, 0), (0, 0), (0, HD - 6)))
    own_scales = lax.dynamic_index_in_dim(scales, yh, 0, False)
    own_text = lax.dynamic_index_in_dim(text_kv, yh, 1, False)
    far_scales = lax.dynamic_index_in_dim(scales, 1 - yh, 0, False)
    far_text = lax.dynamic_index_in_dim(text_kv, 1 - yh, 1, False)
    package = jnp.concatenate(
        [
            sent,
            jnp.pad(far_text.reshape(16, 384), ((0, 0), (0, HD))),
            jnp.pad(far_scales, ((0, 0), (0, 512 - HD))),
        ],
        axis=0,
    )
    package = lax.ppermute(package, "yh", [(0, 1), (1, 0)])
    received, got_text, got_scales = package[:48], package[48:64, :384], package[64:, :HD]
    both_scales = jnp.where(
        lower,
        jnp.concatenate([own_scales, got_scales]),
        jnp.concatenate([got_scales, own_scales]),
    )
    both_text = jnp.concatenate([own_text, got_text.reshape(2, 8, 384)], axis=1)

    line = jnp.concatenate(
        [kept, received, by_part[1][:, HD : 2 * HD], jnp.transpose(w_out)], axis=1
    )
    weights = lax.all_to_all(jnp.broadcast_to(line, (8, 48, 1536)), Z, 0, 0, tiled=True)

    rows = jnp.concatenate(
        [
            image_hidden.reshape(128, 768),
            picked[:, :2].reshape(4, 768),
            jnp.zeros((12, 768), jnp.bfloat16),
        ],
        axis=0,
    )
    rows = lax.all_gather(rows, H, axis=0)
    normed = call(norm_kernel, shape(8, 128, 768), (rows,))
    normed = lax.all_to_all(normed, YX, 0, 0, tiled=True)

    partial = call(
        project_kernel, shape(8, 128, 640), (normed, weights), flops=2 * 1024 * 768 * 576
    )
    partial = lax.all_to_all(partial, YX, 0, 0, tiled=True)

    w_columns = weights[:, :, 1152:].reshape(384, 384)
    w_columns = lax.all_to_all(jnp.broadcast_to(w_columns, (8, 384, 384)), YX, 0, 0, tiled=True)

    own_prev = lax.dynamic_index_in_dim(prev_kv, yh, 1, False)
    first = (8 * x + z) * 64
    earlier = jnp.concatenate(
        [
            lax.dynamic_slice_in_dim(own_prev, first, 64, 1),
            lax.dynamic_slice_in_dim(own_prev, first + 2048, 64, 1),
        ],
        axis=1,
    )
    queries, kv_pair = call(
        restore_kernel,
        (shape(128, 384), shape(8, 288, 384)),
        (partial, earlier, both_scales, both_text, q_gain.reshape(1, HD), k_gain.reshape(1, HD)),
    )
    far_queries = [
        lax.ppermute(queries, "zo", [(i, (i + k) % 4) for i in range(4)]) for k in (1, 2, 3)
    ]
    kv_pair = lax.all_to_all(kv_pair, ("x", "zi"), 0, 0, tiled=True)
    mixed = call(
        attend_kernel,
        (shape(128, 512),) * 4,
        (queries, *far_queries, kv_pair),
        flops=4 * 512 * 1152 * 384,
    )
    mixed = [mixed[0]] + [
        lax.ppermute(mixed[k], "zo", [(i, (i - k) % 4) for i in range(4)]) for k in (1, 2, 3)
    ]
    products = call(
        output_kernel,
        shape(8, 64, 768),
        (*mixed, w_columns),
        scratch=[pltpu.VMEM((128, 384), jnp.bfloat16)],
        flops=2 * 128 * 384 * 3072,
    )
    products = lax.all_to_all(products, ("yh",) + H, 0, 0, tiled=True)
    return call(gate_kernel, shape(2, 64, 768), (products, picked[:, 2]))


def solution(mesh):
    names = ("yh", "x", "zo", "zi", "yl", "c")
    fine = Mesh(mesh.devices.reshape(2, 4, 4, 2, 2, 2), names)
    patch, head = ("yh", "x", "zo", "zi"), ("yl", "c")
    placed = (
        P(None, patch, head),
        P(None, None, patch, head),
        P(None, None, None, head),
        P(None, None, patch, head),
        P(patch, None, head),
        P(head, patch),
        P(None, None, head),
        P(),
        P(),
        P(),
    )
    return jax.shard_map(
        per_device, mesh=fine, in_specs=placed, out_specs=P(None, patch, head), check_vma=False
    )
```

```python
import jax
import jax.numpy as jnp
from jax import lax
from jax.experimental import pallas as pl
from jax.experimental.pallas import tpu as pltpu
from jax.sharding import Mesh, PartitionSpec as P

HD = 128
EPSILON = 1e-06
CODE_LIMIT = 448.0
LOG2E = 1.4426950408889634
VMEM_BYTES = 16 * 1024 * 1024

YX = ("yh", "x")
Z = ("zo", "zi")
H = ("yl", "c")


def call(kernel, out_shapes, operands, scratch=(), scalars=(), flops=0, limit=VMEM_BYTES):
    return pl.pallas_call(
        kernel,
        out_shape=out_shapes,
        in_specs=[
            pl.BlockSpec(memory_space=pltpu.SMEM if at in scalars else pltpu.VMEM)
            for at in range(len(operands))
        ],
        out_specs=jax.tree.map(lambda _: pl.BlockSpec(memory_space=pltpu.VMEM), out_shapes),
        scratch_shapes=scratch,
        compiler_params=pltpu.CompilerParams(vmem_limit_bytes=limit),
        cost_estimate=pl.CostEstimate(flops=flops, bytes_accessed=0, transcendentals=0),
    )(*operands)


def pack_kernel(hidden_ref, table_ref, steps_ref, rows_ref, gate_ref):
    rows_ref[0:128, :] = hidden_ref[...]
    plan = table_ref.shape[1]
    point = lax.broadcasted_iota(jnp.int32, (plan, 768), 0)
    row = lax.broadcasted_iota(jnp.int32, (16, 768), 0)
    modulation = jnp.zeros((16, 768), jnp.float32)
    gates = jnp.zeros((16, 768), jnp.float32)
    for image in range(2):
        chosen = point == steps_ref[image]
        for part in range(3):
            line = jnp.sum(
                jnp.where(chosen, table_ref[part].astype(jnp.float32), 0.0), axis=0, keepdims=True
            )
            if part < 2:
                modulation = jnp.where(row == 2 * image + part, line, modulation)
            else:
                gates = jnp.where(row == image, line, gates)
    rows_ref[128:144, :] = modulation.astype(jnp.bfloat16)
    gate_ref[...] = gates


def norm_kernel(rows_ref, out_ref):
    features = 4 * 768
    for image in range(2):
        shift = rows_ref[:, 128 + 2 * image : 129 + 2 * image, :].astype(jnp.float32)
        scale = 1.0 + rows_ref[:, 129 + 2 * image : 130 + 2 * image, :].astype(jnp.float32)
        for start in range(0, 64, 16):
            at = image * 64 + start
            hidden = rows_ref[:, at : at + 16, :].astype(jnp.float32)
            centre = jnp.sum(jnp.sum(hidden, axis=0), axis=-1, keepdims=True) / features
            off = hidden - centre[None]
            variance = jnp.sum(jnp.sum(off * off, axis=0), axis=-1, keepdims=True) / features
            normed = (off * lax.rsqrt(variance + EPSILON)[None] * scale + shift).astype(jnp.bfloat16)
            for y in range(2):
                for x in range(4):
                    for place, block in enumerate((4 * y + x, 4 * (1 - y) + x)):
                        piece = normed[block // 2][:, (block % 2) * 384 : (block % 2) * 384 + 384]
                        out_ref[4 * y + x, at : at + 16, place * 384 : place * 384 + 384] = piece


def project_kernel(rows_ref, weights_ref, out_ref, columns_ref):
    weights = weights_ref[...].reshape(384, 1536)
    columns_ref[...] = weights[:, 1152:]
    for x in range(4):
        rows = jnp.concatenate([rows_ref[x], rows_ref[4 + x]], axis=0)
        own, other = rows[:, :384], rows[:, 384:]
        most = jnp.dot(own, weights[:, :512], preferred_element_type=jnp.float32) + jnp.dot(
            other, weights[:, 512:1024], preferred_element_type=jnp.float32
        )
        rest = jnp.dot(own, weights[:, 1024:1152], preferred_element_type=jnp.float32)
        both = jnp.concatenate([most, rest], axis=1).astype(jnp.bfloat16)
        for image in range(2):
            for y in range(2):
                piece = both[y * 128 + image * 64 : y * 128 + image * 64 + 64]
                out_ref[4 * image + x, y * 64 : y * 64 + 64, :] = piece


def rms_scale(vectors, gain):
    return vectors * lax.rsqrt(jnp.mean(vectors * vectors, axis=-1, keepdims=True) + EPSILON) * gain


def summed(part_ref, sources, at):
    acc = part_ref[sources[0], :, at : at + HD].astype(jnp.float32)
    for source in sources[1:]:
        acc = acc + part_ref[source, :, at : at + HD].astype(jnp.float32)
    return acc


LOW, HIGH = (0, 1, 2, 3), (4, 5, 6, 7)


def query_kernel(part_ref, q_gain_ref, q_ref):
    for head in range(3):
        lanes = slice(head * HD, head * HD + HD)
        q_ref[:, lanes] = rms_scale(summed(part_ref, LOW, head * HD), q_gain_ref[...]).astype(
            jnp.bfloat16
        )


def restore_kernel(part_ref, prev_ref, kept_ref, got_ref, k_gain_ref, y_ref, kv_ref):
    lower = y_ref[0] == 0
    key_places = ((LOW, 384), (LOW + HIGH, 512), (HIGH, 384))
    kept, got = (ref[16:80, 0:HD].astype(jnp.float32) for ref in (kept_ref, got_ref))
    scales = jnp.concatenate([jnp.where(lower, kept, got), jnp.where(lower, got, kept)], axis=0)

    def restored(fresh, kind, head):
        earlier = prev_ref[kind, :, head * HD : head * HD + HD].astype(jnp.float32)
        lane = kind * 3 + head
        scale = scales[:, lane : lane + 1]
        limit = CODE_LIMIT * scale
        scaled = jnp.clip(fresh - earlier, -limit, limit).astype(jnp.bfloat16).astype(jnp.float32)
        return (earlier + scaled).astype(jnp.bfloat16)

    for head in range(3):
        lanes = slice(head * HD, head * HD + HD)
        keys = restored(rms_scale(summed(part_ref, *key_places[head]), k_gain_ref[...]), 0, head)
        values = restored(summed(part_ref, HIGH, head * HD), 1, head)
        for peer in range(8):
            kv_ref[peer, 0:128, lanes] = keys
            kv_ref[peer, 144:272, lanes] = values
    own, far = (ref[0:16, :].astype(jnp.float32) for ref in (kept_ref, got_ref))
    for kind in range(2):
        text = jnp.concatenate([own[8 * kind : 8 * kind + 8], far[8 * kind : 8 * kind + 8]], axis=0)
        text = text.astype(jnp.bfloat16)
        for peer in range(8):
            kv_ref[peer, 128 + 144 * kind : 144 + 144 * kind, :] = text


def split_three(value):
    first = value.astype(jnp.bfloat16)
    rest = value - first.astype(jnp.float32)
    second = rest.astype(jnp.bfloat16)
    third = (rest - second.astype(jnp.float32)).astype(jnp.bfloat16)
    return first, second, third


def attend_kernel(q0_ref, q1_ref, q2_ref, q3_ref, kv_ref, o0_ref, o1_ref, o2_ref, o3_ref):
    factor = LOG2E * HD**-0.5
    lane = lax.broadcasted_iota(jnp.int32, (128, HD), 1)
    stats = [jnp.zeros((128, HD), jnp.float32) for _ in range(4)]
    for head in range(3):
        lanes = slice(head * HD, head * HD + HD)
        keys = kv_ref[:, 0:144, lanes].reshape(1152, HD)
        values = kv_ref[:, 144:288, lanes].reshape(1152, HD)
        for block, (q_ref, o_ref) in enumerate(
            ((q0_ref, o0_ref), (q1_ref, o1_ref), (q2_ref, o2_ref), (q3_ref, o3_ref))
        ):
            logits = lax.dot_general(
                q_ref[:, lanes], keys, (((1,), (1,)), ((), ())), preferred_element_type=jnp.float32
            )
            peak = jnp.max(logits, axis=-1, keepdims=True)
            terms = jnp.exp2((logits - peak) * factor)
            total = jnp.sum(terms, axis=-1, keepdims=True)
            mixed = jnp.dot(terms.astype(jnp.bfloat16), values, preferred_element_type=jnp.float32)
            o_ref[:, lanes] = (mixed / total).astype(jnp.bfloat16)
            for place, part in enumerate(split_three(peak * factor + jnp.log2(total))):
                stats[block] = jnp.where(
                    lane == head * 3 + place, part.astype(jnp.float32), stats[block]
                )
    for block, o_ref in enumerate((o0_ref, o1_ref, o2_ref, o3_ref)):
        o_ref[:, 384:512] = stats[block].astype(jnp.bfloat16)


def combine_kernel(p0_ref, p1_ref, p2_ref, p3_ref, y_ref, kept_ref, sent_ref):
    parts = (p0_ref, p1_ref, p2_ref, p3_ref)
    lower = y_ref[0] == 0
    stats = [ref[:, 384:512].astype(jnp.float32) for ref in parts]
    for head in range(3):
        lanes = slice(head * HD, head * HD + HD)
        sizes = [
            stat[:, head * 3 : head * 3 + 1]
            + stat[:, head * 3 + 1 : head * 3 + 2]
            + stat[:, head * 3 + 2 : head * 3 + 3]
            for stat in stats
        ]
        top = jnp.maximum(jnp.maximum(sizes[0], sizes[1]), jnp.maximum(sizes[2], sizes[3]))
        shares = [jnp.exp2(size - top) for size in sizes]
        whole = shares[0] + shares[1] + shares[2] + shares[3]
        mixed = shares[0] * parts[0][:, lanes].astype(jnp.float32)
        for share, ref in zip(shares[1:], parts[1:]):
            mixed = mixed + share * ref[:, lanes].astype(jnp.float32)
        mixed = (mixed / whole).astype(jnp.bfloat16)
        kept_ref[:, lanes] = jnp.where(lower, mixed[:64], mixed[64:])
        sent_ref[:, lanes] = jnp.where(lower, mixed[64:], mixed[:64])


def output_kernel(attended_ref, weights_ref, gate_ref, out_ref):
    for half in range(2):
        lanes = slice(half * 384, half * 384 + 384)
        sums = jnp.zeros((128, 384), jnp.float32)
        for group in range(4):
            sums = sums + lax.dot_general(
                attended_ref[group],
                weights_ref[half, group],
                (((1,), (1,)), ((), ())),
                preferred_element_type=jnp.float32,
            )
        for image in range(2):
            rows = gate_ref[image : image + 1, lanes] * sums[64 * image : 64 * image + 64]
            out_ref[image, :, lanes] = rows.astype(jnp.bfloat16)


def power_two(exponents):
    summed = jnp.zeros(exponents.shape, jnp.float32)
    for exponent in range(-8, 1):
        summed = summed + jnp.where(exponents == exponent, jnp.float32(2.0**exponent), 0.0)
    return summed


def shape(*dims):
    return jax.ShapeDtypeStruct(dims, jnp.bfloat16)


def column_moves():
    moves = []
    for y in range(2):
        for x in range(4):
            for head in range(4):
                moves.append(((y * 4 + x) * 4 + head, ((x % 2) * 4 + head) * 4 + 2 * y + x // 2))
    return moves


def per_device(
    image_hidden, text_kv, prev_kv, scale_exp, w_qkv, w_out, mod_table, timesteps, q_gain, k_gain
):
    yh, x = lax.axis_index("yh"), lax.axis_index("x")
    z = lax.axis_index(Z)
    lower = yh == 0
    y_at = yh.reshape(1)
    by_part = jnp.transpose(w_qkv, (1, 0, 2))
    for_low = jnp.concatenate([by_part[0], by_part[1][:, :HD]], axis=1)
    for_high = jnp.concatenate([by_part[2], by_part[1][:, 2 * HD :]], axis=1)
    kept, sent = jnp.where(lower, for_low, for_high), jnp.where(lower, for_high, for_low)
    swap = [(0, 1), (1, 0)]
    got = lax.ppermute(sent, "yh", swap)
    columns = lax.ppermute(jnp.transpose(w_out), ("yh", "x") + H, column_moves())

    rows, gates = call(
        pack_kernel,
        (shape(144, 768), jax.ShapeDtypeStruct((16, 768), jnp.float32)),
        (image_hidden.reshape(128, 768), jnp.transpose(mod_table, (1, 0, 2)), timesteps),
        scalars=(2,),
        limit=4 * VMEM_BYTES - 8 * 1024 * 1024,
    )

    line = jnp.concatenate([kept, got, by_part[1][:, HD : 2 * HD], columns], axis=1)
    line, rows = lax.optimization_barrier((line, rows))
    weights = lax.all_gather(line, Z, axis=0)

    scales = jnp.transpose(power_two(scale_exp), (1, 2, 0, 3)).reshape(2, 64, 6).astype(jnp.bfloat16)
    scales = jnp.pad(scales, ((0, 0), (0, 0), (0, 384 - 6)))
    text = jnp.transpose(text_kv, (1, 0, 2, 3)).reshape(2, 16, 384)
    package = jnp.concatenate([text, scales], axis=1)
    own_package = jnp.where(lower, package[0], package[1])
    far_package = lax.ppermute(jnp.where(lower, package[1], package[0]), "yh", swap)

    rows = lax.all_gather(rows, H, axis=0)
    rows, far_package = lax.optimization_barrier((rows, far_package))
    normed = call(norm_kernel, shape(8, 128, 768), (rows,))
    normed = lax.all_to_all(normed, YX, 0, 0, tiled=True)

    partial, columns = call(
        project_kernel,
        (shape(8, 128, 640), shape(384, 384)),
        (normed, weights),
        flops=2 * 1024 * 768 * 576,
    )
    partial = lax.all_to_all(partial, YX, 0, 0, tiled=True)
    columns = lax.all_gather(columns, YX, axis=0)

    own_prev = lax.dynamic_index_in_dim(prev_kv, yh, 1, False)
    first = (8 * x + z) * 64
    earlier = jnp.concatenate(
        [
            lax.dynamic_slice_in_dim(own_prev, first, 64, 1),
            lax.dynamic_slice_in_dim(own_prev, first + 2048, 64, 1),
        ],
        axis=1,
    )
    queries = call(query_kernel, shape(128, 384), (partial, q_gain.reshape(1, HD)))
    far_queries = [
        lax.ppermute(queries, "zo", [(i, (i + k) % 4) for i in range(4)]) for k in (1, 2, 3)
    ]
    kv_pair = call(
        restore_kernel,
        shape(8, 288, 384),
        (partial, earlier, own_package, far_package, k_gain.reshape(1, HD), y_at),
        scalars=(5,),
    )
    kv_pair = lax.all_to_all(kv_pair, ("x", "zi"), 0, 0, tiled=True)
    mixed = call(
        attend_kernel,
        (shape(128, 512),) * 4,
        (queries, *far_queries, kv_pair),
        flops=4 * 512 * 1152 * 384,
    )
    mixed = [mixed[0]] + [
        lax.ppermute(mixed[k], "zo", [(i, (i - k) % 4) for i in range(4)]) for k in (1, 2, 3)
    ]
    own, far = call(combine_kernel, (shape(64, 384),) * 2, (*mixed, y_at), scalars=(4,))
    far = lax.ppermute(far, "yh", [(0, 1), (1, 0)])
    attended = jnp.where(lower, jnp.concatenate([own, far]), jnp.concatenate([far, own]))
    attended = lax.all_gather(attended, H, axis=0)
    return call(
        output_kernel,
        shape(2, 64, 768),
        (attended, columns.reshape(2, 4, 384, 384), gates),
        flops=2 * 128 * 1536 * 768,
    )


def solution(mesh):
    names = ("yh", "x", "zo", "zi", "yl", "c")
    fine = Mesh(mesh.devices.reshape(2, 4, 4, 2, 2, 2), names)
    patch, head = ("yh", "x", "zo", "zi"), ("yl", "c")
    placed = (
        P(None, patch, head),
        P(None, None, patch, head),
        P(None, None, None, head),
        P(None, None, patch, head),
        P(patch, None, head),
        P(head, patch),
        P(None, None, head),
        P(),
        P(),
        P(),
    )
    return jax.shard_map(
        per_device, mesh=fine, in_specs=placed, out_specs=P(None, patch, head), check_vma=False
    )
```

```python
import jax
import jax.numpy as jnp
from jax import lax
from jax.experimental import pallas as pl
from jax.experimental.pallas import tpu as pltpu
from jax.sharding import Mesh, PartitionSpec as P

HD = 128
EPSILON = 1e-06
CODE_LIMIT = 448.0
LOG2E = 1.4426950408889634
VMEM_BYTES = 16 * 1024 * 1024
WIDE_BYTES = 58 * 1024 * 1024

X = ("xj", "xi")
YX = ("yh",) + X
Z = ("zo", "zi")
H = ("yl", "c")


def call(kernel, out_shapes, operands, scratch=(), scalars=(), flops=0, limit=VMEM_BYTES):
    return pl.pallas_call(
        kernel,
        out_shape=out_shapes,
        in_specs=[
            pl.BlockSpec(memory_space=pltpu.SMEM if at in scalars else pltpu.VMEM)
            for at in range(len(operands))
        ],
        out_specs=jax.tree.map(lambda _: pl.BlockSpec(memory_space=pltpu.VMEM), out_shapes),
        scratch_shapes=scratch,
        compiler_params=pltpu.CompilerParams(vmem_limit_bytes=limit),
        cost_estimate=pl.CostEstimate(flops=flops, bytes_accessed=0, transcendentals=0),
    )(*operands)


def pack_kernel(hidden_ref, table_ref, steps_ref, rows_ref, gate_ref):
    rows_ref[0:128, :] = hidden_ref[...]
    plan = table_ref.shape[1]
    point = lax.broadcasted_iota(jnp.int32, (plan, 768), 0)
    row = lax.broadcasted_iota(jnp.int32, (16, 768), 0)
    modulation = jnp.zeros((16, 768), jnp.float32)
    gates = jnp.zeros((16, 768), jnp.float32)
    for image in range(2):
        chosen = point == steps_ref[image]
        for part in range(3):
            line = jnp.sum(
                jnp.where(chosen, table_ref[part].astype(jnp.float32), 0.0), axis=0, keepdims=True
            )
            if part < 2:
                modulation = jnp.where(row == 2 * image + part, line, modulation)
            else:
                gates = jnp.where(row == image, line, gates)
    rows_ref[128:144, :] = modulation.astype(jnp.bfloat16)
    gate_ref[...] = gates


def norm_kernel(rows_ref, y_ref, out_ref):
    features = 4 * 768
    lower = y_ref[0] == 0
    for image in range(2):
        shift = rows_ref[:, 128 + 2 * image : 129 + 2 * image, :].astype(jnp.float32)
        scale = 1.0 + rows_ref[:, 129 + 2 * image : 130 + 2 * image, :].astype(jnp.float32)
        for start in range(0, 64, 16):
            at = image * 64 + start
            hidden = rows_ref[:, at : at + 16, :].astype(jnp.float32)
            centre = jnp.sum(jnp.sum(hidden, axis=0), axis=-1, keepdims=True) / features
            off = hidden - centre[None]
            variance = jnp.sum(jnp.sum(off * off, axis=0), axis=-1, keepdims=True) / features
            normed = (off * lax.rsqrt(variance + EPSILON)[None] * scale + shift).astype(jnp.bfloat16)
            for x in range(4):
                lanes = slice((x % 2) * 384, (x % 2) * 384 + 384)
                low, high = normed[x // 2][:, lanes], normed[2 + x // 2][:, lanes]
                out_ref[x, at : at + 16, 0:384] = jnp.where(lower, low, high)
                out_ref[x, at : at + 16, 384:768] = jnp.where(lower, high, low)


def column_kernel(weights_ref, columns_ref):
    step = pl.program_id(0)

    @pl.when(step == 0)
    def _():
        columns_ref[:, :, 0:128] = weights_ref[:, 0:48, :]

    @pl.when(step == 1)
    def _():
        columns_ref[:, :, 128:256] = weights_ref[:, 0:48, :]
        columns_ref[:, :, 256:384] = weights_ref[:, 48:96, :]


def project_kernel(rows_ref, weights_ref, out_ref):
    for part in range(3):
        lanes = slice(part * 384, part * 384 + 384)
        sums = jnp.zeros((512, 384), jnp.float32)
        for y in range(2):
            sums = sums + jnp.dot(
                rows_ref[:, :, y * 384 : y * 384 + 384].reshape(512, 384),
                weights_ref[:, y * 48 : y * 48 + 48, lanes].reshape(384, 384),
                preferred_element_type=jnp.float32,
            )
        for x in range(4):
            for image in range(2):
                at = x * 128 + image * 64
                place = (x % 2) * 64
                out_ref[(x // 2) * 2 + image, place : place + 64, lanes] = sums[
                    at : at + 64
                ].astype(jnp.bfloat16)


def rms_scale(vectors, gain):
    return vectors * lax.rsqrt(jnp.mean(vectors * vectors, axis=-1, keepdims=True) + EPSILON) * gain


def summed(part_ref, at):
    acc = part_ref[0, :, at : at + HD].astype(jnp.float32)
    for source in range(1, 4):
        acc = acc + part_ref[source, :, at : at + HD].astype(jnp.float32)
    return acc


def query_kernel(part_ref, q_gain_ref, q_ref):
    for head in range(3):
        lanes = slice(head * HD, head * HD + HD)
        q_ref[:, lanes] = rms_scale(summed(part_ref, head * HD), q_gain_ref[...]).astype(
            jnp.bfloat16
        )


def restore_kernel(part_ref, prev_ref, kept_ref, got_ref, k_gain_ref, image_ref, kv_ref):
    first = image_ref[0] == 0
    kept, got = (ref[16:80, 0:HD].astype(jnp.float32) for ref in (kept_ref, got_ref))
    scales = jnp.concatenate([jnp.where(first, kept, got), jnp.where(first, got, kept)], axis=0)

    def restored(fresh, kind, head):
        earlier = prev_ref[kind, :, head * HD : head * HD + HD].astype(jnp.float32)
        lane = kind * 3 + head
        scale = scales[:, lane : lane + 1]
        limit = CODE_LIMIT * scale
        scaled = jnp.clip(fresh - earlier, -limit, limit).astype(jnp.bfloat16).astype(jnp.float32)
        return (earlier + scaled).astype(jnp.bfloat16)

    for head in range(3):
        lanes = slice(head * HD, head * HD + HD)
        keys = rms_scale(summed(part_ref, 384 + head * HD), k_gain_ref[...])
        kv_ref[0:128, lanes] = restored(keys, 0, head)
        kv_ref[144:272, lanes] = restored(summed(part_ref, 768 + head * HD), 1, head)
    own, far = (ref[0:16, :].astype(jnp.float32) for ref in (kept_ref, got_ref))
    for kind in range(2):
        text = jnp.concatenate([own[8 * kind : 8 * kind + 8], far[8 * kind : 8 * kind + 8]], axis=0)
        kv_ref[128 + 144 * kind : 144 + 144 * kind, :] = text.astype(jnp.bfloat16)


def split_three(value):
    first = value.astype(jnp.bfloat16)
    rest = value - first.astype(jnp.float32)
    second = rest.astype(jnp.bfloat16)
    third = (rest - second.astype(jnp.float32)).astype(jnp.bfloat16)
    return first, second, third


def attend_kernel(q0_ref, q1_ref, q2_ref, q3_ref, kv_ref, o0_ref, o1_ref, o2_ref, o3_ref):
    factor = LOG2E * HD**-0.5
    lane = lax.broadcasted_iota(jnp.int32, (128, HD), 1)
    stats = [jnp.zeros((128, HD), jnp.float32) for _ in range(4)]
    for head in range(3):
        lanes = slice(head * HD, head * HD + HD)
        keys = kv_ref[:, 0:144, lanes].reshape(1152, HD)
        values = kv_ref[:, 144:288, lanes].reshape(1152, HD)
        for block, (q_ref, o_ref) in enumerate(
            ((q0_ref, o0_ref), (q1_ref, o1_ref), (q2_ref, o2_ref), (q3_ref, o3_ref))
        ):
            logits = lax.dot_general(
                q_ref[:, lanes], keys, (((1,), (1,)), ((), ())), preferred_element_type=jnp.float32
            )
            peak = jnp.max(logits, axis=-1, keepdims=True)
            terms = jnp.exp2((logits - peak) * factor)
            total = jnp.sum(terms, axis=-1, keepdims=True)
            mixed = jnp.dot(terms.astype(jnp.bfloat16), values, preferred_element_type=jnp.float32)
            o_ref[:, lanes] = (mixed / total).astype(jnp.bfloat16)
            for place, part in enumerate(split_three(peak * factor + jnp.log2(total))):
                stats[block] = jnp.where(
                    lane == head * 3 + place, part.astype(jnp.float32), stats[block]
                )
    for block, o_ref in enumerate((o0_ref, o1_ref, o2_ref, o3_ref)):
        o_ref[:, 384:512] = stats[block].astype(jnp.bfloat16)


def combine_kernel(p0_ref, p1_ref, p2_ref, p3_ref, image_ref, kept_ref, sent_ref):
    parts = (p0_ref, p1_ref, p2_ref, p3_ref)
    first = image_ref[0] == 0
    stats = [ref[:, 384:512].astype(jnp.float32) for ref in parts]
    for head in range(3):
        lanes = slice(head * HD, head * HD + HD)
        sizes = [
            stat[:, head * 3 : head * 3 + 1]
            + stat[:, head * 3 + 1 : head * 3 + 2]
            + stat[:, head * 3 + 2 : head * 3 + 3]
            for stat in stats
        ]
        top = jnp.maximum(jnp.maximum(sizes[0], sizes[1]), jnp.maximum(sizes[2], sizes[3]))
        shares = [jnp.exp2(size - top) for size in sizes]
        whole = shares[0] + shares[1] + shares[2] + shares[3]
        mixed = shares[0] * parts[0][:, lanes].astype(jnp.float32)
        for share, ref in zip(shares[1:], parts[1:]):
            mixed = mixed + share * ref[:, lanes].astype(jnp.float32)
        mixed = (mixed / whole).astype(jnp.bfloat16)
        kept_ref[:, lanes] = jnp.where(first, mixed[:64], mixed[64:])
        sent_ref[:, lanes] = jnp.where(first, mixed[64:], mixed[:64])


def output_kernel(attended_ref, weights_ref, gate_ref, out_ref):
    for half in range(2):
        lanes = slice(half * 384, half * 384 + 384)
        sums = jnp.zeros((128, 384), jnp.float32)
        for group in range(4):
            sums = sums + lax.dot_general(
                attended_ref[group],
                weights_ref[group, half].reshape(384, 384),
                (((1,), (1,)), ((), ())),
                preferred_element_type=jnp.float32,
            )
        for image in range(2):
            rows = gate_ref[image : image + 1, lanes] * sums[64 * image : 64 * image + 64]
            out_ref[image, :, lanes] = rows.astype(jnp.bfloat16)


def power_two(exponents):
    summed = jnp.zeros(exponents.shape, jnp.float32)
    for exponent in range(-8, 1):
        summed = summed + jnp.where(exponents == exponent, jnp.float32(2.0**exponent), 0.0)
    return summed


def shape(*dims):
    return jax.ShapeDtypeStruct(dims, jnp.bfloat16)


def column_moves():
    moves = []
    for yh in range(2):
        for x in range(4):
            for yl in range(2):
                for c in range(2):
                    there = ((yl * 4 + 2 * c + x % 2) * 2 + yh) * 2 + x // 2
                    moves.append((((yh * 4 + x) * 2 + yl) * 2 + c, there))
    return moves


def per_device(
    image_hidden, text_kv, prev_kv, scale_exp, w_qkv, w_out, mod_table, timesteps, q_gain, k_gain
):
    yh, xj, xi = (lax.axis_index(name) for name in YX)
    z = lax.axis_index(Z)
    first = xi == 0
    image_at = xi.reshape(1)
    swap = [(0, 1), (1, 0)]
    by_part = jnp.transpose(w_qkv, (1, 0, 2))
    got = lax.ppermute(by_part, "yh", swap)

    rows, gates = call(
        pack_kernel,
        (shape(144, 768), jax.ShapeDtypeStruct((16, 768), jnp.float32)),
        (image_hidden.reshape(128, 768), jnp.transpose(mod_table, (1, 0, 2)), timesteps),
        scalars=(2,),
        limit=WIDE_BYTES,
    )

    columns = lax.ppermute(jnp.transpose(w_out), YX + H, column_moves())

    line = jnp.concatenate(
        [
            jnp.concatenate([by_part[0], by_part[1], by_part[2], columns[:, :256]], axis=1),
            jnp.concatenate([got[0], got[1], got[2], columns[:, 128:]], axis=1),
        ],
        axis=0,
    )
    line, rows = lax.optimization_barrier((line, rows))
    weights = lax.all_gather(line, Z, axis=0)

    scales = jnp.transpose(power_two(scale_exp), (1, 2, 0, 3)).reshape(2, 64, 6).astype(jnp.bfloat16)
    scales = jnp.pad(scales, ((0, 0), (0, 0), (0, 384 - 6)))
    text = jnp.transpose(text_kv, (1, 0, 2, 3)).reshape(2, 16, 384)
    package = jnp.concatenate([text, scales], axis=1)
    own_package = jnp.where(first, package[0], package[1])
    far_package = lax.ppermute(jnp.where(first, package[1], package[0]), "xi", swap)
    rows = lax.all_gather(rows, H, axis=0)
    rows, far_package = lax.optimization_barrier((rows, far_package))
    normed = call(norm_kernel, shape(4, 128, 768), (rows, yh.reshape(1)), scalars=(1,))
    normed = lax.all_to_all(normed, X, 0, 0, tiled=True)
    columns = pl.pallas_call(
        column_kernel,
        out_shape=shape(8, 48, 384),
        grid=(2,),
        in_specs=[pl.BlockSpec((8, 96, HD), lambda step: (0, 0, 9 + step))],
        out_specs=pl.BlockSpec((8, 48, 384), lambda step: (0, 0, 0)),
        compiler_params=pltpu.CompilerParams(vmem_limit_bytes=WIDE_BYTES),
    )(weights)
    normed, columns = lax.optimization_barrier((normed, columns))
    columns = lax.all_gather(columns, YX, axis=0)
    partial = call(
        project_kernel, shape(4, 128, 1152), (normed, weights), flops=2 * 512 * 768 * 1152
    )
    partial = lax.all_to_all(partial, X, 0, 0, tiled=True)

    own_prev = lax.dynamic_index_in_dim(prev_kv, xi, 1, False)
    start = (32 * yh + 16 * xj + z) * 64
    earlier = jnp.concatenate(
        [
            lax.dynamic_slice_in_dim(own_prev, start, 64, 1),
            lax.dynamic_slice_in_dim(own_prev, start + 512, 64, 1),
        ],
        axis=1,
    )
    queries = call(query_kernel, shape(128, 384), (partial, q_gain.reshape(1, HD)))
    kv_pair = call(
        restore_kernel,
        shape(288, 384),
        (partial, earlier, own_package, far_package, k_gain.reshape(1, HD), image_at),
        scalars=(5,),
    )
    kv_pair = jnp.stack([kv_pair, lax.ppermute(kv_pair, "zi", swap)])
    far_queries = [
        lax.ppermute(queries, "zo", [(i, (i + k) % 4) for i in range(4)]) for k in (1, 2, 3)
    ]
    kv_pair = lax.all_to_all(
        jnp.broadcast_to(kv_pair, (4, 2, 288, 384)), ("yh", "xj"), 0, 0, tiled=True
    ).reshape(8, 288, 384)
    mixed = call(
        attend_kernel,
        (shape(128, 512),) * 4,
        (queries, *far_queries, kv_pair),
        flops=4 * 512 * 1152 * 384,
    )
    mixed = [mixed[0]] + [
        lax.ppermute(mixed[k], "zo", [(i, (i - k) % 4) for i in range(4)]) for k in (1, 2, 3)
    ]
    own, far = call(combine_kernel, (shape(64, 384),) * 2, (*mixed, image_at), scalars=(4,))
    far = lax.ppermute(far, "xi", swap)
    attended = jnp.where(first, jnp.concatenate([own, far]), jnp.concatenate([far, own]))
    attended = lax.all_gather(attended, H, axis=0)
    return call(
        output_kernel,
        shape(2, 64, 768),
        (attended, columns.reshape(4, 2, 8, 48, 384), gates),
        flops=2 * 128 * 1536 * 768,
    )


def solution(mesh):
    names = ("yh", "xj", "xi", "zo", "zi", "yl", "c")
    fine = Mesh(mesh.devices.reshape(2, 2, 2, 4, 2, 2, 2), names)
    patch, head = YX + Z, H
    placed = (
        P(None, patch, head),
        P(None, None, patch, head),
        P(None, None, None, head),
        P(None, None, patch, head),
        P(patch, None, head),
        P(head, patch),
        P(None, None, head),
        P(),
        P(),
        P(),
    )
    return jax.shard_map(
        per_device, mesh=fine, in_specs=placed, out_specs=P(None, patch, head), check_vma=False
    )
```

```python
import jax
import jax.numpy as jnp
from jax import lax
from jax.experimental import pallas as pl
from jax.experimental.pallas import tpu as pltpu
from jax.sharding import Mesh, PartitionSpec as P

HD = 128
EPSILON = 1e-06
CODE_LIMIT = 448.0
LOG2E = 1.4426950408889634
VMEM_BYTES = 16 * 1024 * 1024
WIDE_BYTES = 58 * 1024 * 1024

X = ("xj", "xi")
YX = ("yh",) + X
Z = ("zo", "zi")
H = ("yl", "c")


def call(kernel, out_shapes, operands, scratch=(), scalars=(), far=(), flops=0, limit=VMEM_BYTES):
    return pl.pallas_call(
        kernel,
        out_shape=out_shapes,
        in_specs=[
            pl.BlockSpec(
                memory_space=pltpu.SMEM if at in scalars else pltpu.HBM if at in far else pltpu.VMEM
            )
            for at in range(len(operands))
        ],
        out_specs=jax.tree.map(lambda _: pl.BlockSpec(memory_space=pltpu.VMEM), out_shapes),
        scratch_shapes=scratch,
        compiler_params=pltpu.CompilerParams(vmem_limit_bytes=limit),
        cost_estimate=pl.CostEstimate(flops=flops, bytes_accessed=0, transcendentals=0),
    )(*operands)


def pack_kernel(hidden_ref, table_ref, steps_ref, rows_ref, gate_ref):
    rows_ref[0:128, :] = hidden_ref[...]
    plan = table_ref.shape[1]
    point = lax.broadcasted_iota(jnp.int32, (plan, 768), 0)
    row = lax.broadcasted_iota(jnp.int32, (16, 768), 0)
    modulation = jnp.zeros((16, 768), jnp.float32)
    gates = jnp.zeros((16, 768), jnp.float32)
    for image in range(2):
        chosen = point == steps_ref[image]
        for part in range(3):
            line = jnp.sum(
                jnp.where(chosen, table_ref[part].astype(jnp.float32), 0.0), axis=0, keepdims=True
            )
            if part < 2:
                modulation = jnp.where(row == 2 * image + part, line, modulation)
            else:
                gates = jnp.where(row == image, line, gates)
    rows_ref[128:144, :] = modulation.astype(jnp.bfloat16)
    gate_ref[...] = gates


def norm_kernel(rows_ref, y_ref, out_ref):
    features = 4 * 768
    lower = y_ref[0] == 0
    for image in range(2):
        shift = rows_ref[:, 128 + 2 * image : 129 + 2 * image, :].astype(jnp.float32)
        scale = 1.0 + rows_ref[:, 129 + 2 * image : 130 + 2 * image, :].astype(jnp.float32)
        for start in range(0, 64, 16):
            at = image * 64 + start
            hidden = rows_ref[:, at : at + 16, :].astype(jnp.float32)
            centre = jnp.sum(jnp.sum(hidden, axis=0), axis=-1, keepdims=True) / features
            off = hidden - centre[None]
            variance = jnp.sum(jnp.sum(off * off, axis=0), axis=-1, keepdims=True) / features
            normed = (off * lax.rsqrt(variance + EPSILON)[None] * scale + shift).astype(jnp.bfloat16)
            for x in range(4):
                lanes = slice((x % 2) * 384, (x % 2) * 384 + 384)
                low, high = normed[x // 2][:, lanes], normed[2 + x // 2][:, lanes]
                out_ref[x, at : at + 16, 0:384] = jnp.where(lower, low, high)
                out_ref[x, at : at + 16, 384:768] = jnp.where(lower, high, low)


def column_kernel(weights_ref, columns_ref):
    columns_ref[:, :, 0:256] = weights_ref[:, 0:48, :]
    columns_ref[:, :, 256:384] = weights_ref[:, 48:96, 128:256]


def project_kernel(rows_ref, weights_ref, out_ref, held_ref, arrived):
    copies = [
        pltpu.make_async_copy(
            weights_ref.at[:, :, pl.ds(256 + part * 384, 384)], held_ref.at[part], arrived.at[part]
        )
        for part in range(3)
    ]
    for copy in copies:
        copy.start()
    for part in range(3):
        lanes = slice(part * 384, part * 384 + 384)
        copies[part].wait()
        sums = jnp.zeros((512, 384), jnp.float32)
        for y in range(2):
            sums = sums + jnp.dot(
                rows_ref[:, :, y * 384 : y * 384 + 384].reshape(512, 384),
                held_ref[part, :, y * 48 : y * 48 + 48, :].reshape(384, 384),
                preferred_element_type=jnp.float32,
            )
        for x in range(4):
            for image in range(2):
                at = x * 128 + image * 64
                place = (x % 2) * 64
                out_ref[(x // 2) * 2 + image, place : place + 64, lanes] = sums[
                    at : at + 64
                ].astype(jnp.bfloat16)


def rms_scale(vectors, gain):
    return vectors * lax.rsqrt(jnp.mean(vectors * vectors, axis=-1, keepdims=True) + EPSILON) * gain


def summed(part_ref, at):
    acc = part_ref[0, :, at : at + HD].astype(jnp.float32)
    for source in range(1, 4):
        acc = acc + part_ref[source, :, at : at + HD].astype(jnp.float32)
    return acc


def query_kernel(part_ref, q_gain_ref, q_ref):
    for head in range(3):
        lanes = slice(head * HD, head * HD + HD)
        q_ref[:, lanes] = rms_scale(summed(part_ref, head * HD), q_gain_ref[...]).astype(
            jnp.bfloat16
        )


def restore_kernel(part_ref, prev_ref, kept_ref, got_ref, k_gain_ref, image_ref, kv_ref):
    first = image_ref[0] == 0
    kept, got = (ref[16:80, 0:HD].astype(jnp.float32) for ref in (kept_ref, got_ref))
    scales = jnp.concatenate([jnp.where(first, kept, got), jnp.where(first, got, kept)], axis=0)

    def restored(fresh, kind, head):
        earlier = prev_ref[kind, :, head * HD : head * HD + HD].astype(jnp.float32)
        lane = kind * 3 + head
        scale = scales[:, lane : lane + 1]
        limit = CODE_LIMIT * scale
        scaled = jnp.clip(fresh - earlier, -limit, limit).astype(jnp.bfloat16).astype(jnp.float32)
        return (earlier + scaled).astype(jnp.bfloat16)

    for head in range(3):
        lanes = slice(head * HD, head * HD + HD)
        keys = rms_scale(summed(part_ref, 384 + head * HD), k_gain_ref[...])
        kv_ref[0:128, lanes] = restored(keys, 0, head)
        kv_ref[144:272, lanes] = restored(summed(part_ref, 768 + head * HD), 1, head)
    own, far = (ref[0:16, :].astype(jnp.float32) for ref in (kept_ref, got_ref))
    for kind in range(2):
        text = jnp.concatenate([own[8 * kind : 8 * kind + 8], far[8 * kind : 8 * kind + 8]], axis=0)
        kv_ref[128 + 144 * kind : 144 + 144 * kind, :] = text.astype(jnp.bfloat16)


def split_three(value):
    first = value.astype(jnp.bfloat16)
    rest = value - first.astype(jnp.float32)
    second = rest.astype(jnp.bfloat16)
    third = (rest - second.astype(jnp.float32)).astype(jnp.bfloat16)
    return first, second, third


def attend_kernel(q_ref, kv_ref, o_ref):
    factor = LOG2E * HD**-0.5
    lane = lax.broadcasted_iota(jnp.int32, (128, HD), 1)
    stat = jnp.zeros((128, HD), jnp.float32)
    for head in range(3):
        lanes = slice(head * HD, head * HD + HD)
        keys = kv_ref[:, 0:144, lanes].reshape(1152, HD)
        values = kv_ref[:, 144:288, lanes].reshape(1152, HD)
        logits = lax.dot_general(
            q_ref[:, lanes], keys, (((1,), (1,)), ((), ())), preferred_element_type=jnp.float32
        )
        peak = jnp.max(logits, axis=-1, keepdims=True)
        terms = jnp.exp2((logits - peak) * factor)
        total = jnp.sum(terms, axis=-1, keepdims=True)
        mixed = jnp.dot(terms.astype(jnp.bfloat16), values, preferred_element_type=jnp.float32)
        o_ref[0:128, lanes] = (mixed / total).astype(jnp.bfloat16)
        for place, part in enumerate(split_three(peak * factor + jnp.log2(total))):
            stat = jnp.where(lane == head * 3 + place, part.astype(jnp.float32), stat)
    o_ref[128:144, 0:HD] = stat.T[0:16].astype(jnp.bfloat16)
    o_ref[128:144, HD:384] = jnp.zeros((16, 2 * HD), jnp.bfloat16)


def combine_kernel(p0_ref, p1_ref, p2_ref, p3_ref, image_ref, kept_ref, sent_ref):
    parts = (p0_ref, p1_ref, p2_ref, p3_ref)
    first = image_ref[0] == 0
    blank = jnp.zeros((112, HD), jnp.float32)
    stats = [
        jnp.concatenate([ref[128:144, 0:HD].astype(jnp.float32), blank], axis=0).T for ref in parts
    ]
    for head in range(3):
        lanes = slice(head * HD, head * HD + HD)
        sizes = [
            stat[:, head * 3 : head * 3 + 1]
            + stat[:, head * 3 + 1 : head * 3 + 2]
            + stat[:, head * 3 + 2 : head * 3 + 3]
            for stat in stats
        ]
        top = jnp.maximum(jnp.maximum(sizes[0], sizes[1]), jnp.maximum(sizes[2], sizes[3]))
        shares = [jnp.exp2(size - top) for size in sizes]
        whole = shares[0] + shares[1] + shares[2] + shares[3]
        mixed = shares[0] * parts[0][0:128, lanes].astype(jnp.float32)
        for share, ref in zip(shares[1:], parts[1:]):
            mixed = mixed + share * ref[0:128, lanes].astype(jnp.float32)
        mixed = (mixed / whole).astype(jnp.bfloat16)
        kept_ref[:, lanes] = jnp.where(first, mixed[:64], mixed[64:])
        sent_ref[:, lanes] = jnp.where(first, mixed[64:], mixed[:64])


def output_kernel(attended_ref, weights_ref, gate_ref, out_ref):
    for half in range(2):
        lanes = slice(half * 384, half * 384 + 384)
        sums = jnp.zeros((128, 384), jnp.float32)
        for group in range(4):
            sums = sums + lax.dot_general(
                attended_ref[group],
                weights_ref[group, half].reshape(384, 384),
                (((1,), (1,)), ((), ())),
                preferred_element_type=jnp.float32,
            )
        for image in range(2):
            rows = gate_ref[image : image + 1, lanes] * sums[64 * image : 64 * image + 64]
            out_ref[image, :, lanes] = rows.astype(jnp.bfloat16)


def power_two(exponents):
    summed = jnp.zeros(exponents.shape, jnp.float32)
    for exponent in range(-8, 1):
        summed = summed + jnp.where(exponents == exponent, jnp.float32(2.0**exponent), 0.0)
    return summed


def shape(*dims):
    return jax.ShapeDtypeStruct(dims, jnp.bfloat16)


def column_moves():
    moves = []
    for yh in range(2):
        for x in range(4):
            for yl in range(2):
                for c in range(2):
                    there = ((yl * 4 + 2 * c + x % 2) * 2 + yh) * 2 + x // 2
                    moves.append((((yh * 4 + x) * 2 + yl) * 2 + c, there))
    return moves


def per_device(
    image_hidden, text_kv, prev_kv, scale_exp, w_qkv, w_out, mod_table, timesteps, q_gain, k_gain
):
    yh, xj, xi = (lax.axis_index(name) for name in YX)
    z = lax.axis_index(Z)
    first = xi == 0
    image_at = xi.reshape(1)
    swap = [(0, 1), (1, 0)]
    by_part = jnp.transpose(w_qkv, (1, 0, 2))
    got = lax.ppermute(by_part, "yh", swap)

    rows, gates = call(
        pack_kernel,
        (shape(144, 768), jax.ShapeDtypeStruct((16, 768), jnp.float32)),
        (image_hidden.reshape(128, 768), jnp.transpose(mod_table, (1, 0, 2)), timesteps),
        scalars=(2,),
        limit=WIDE_BYTES,
    )

    columns = lax.ppermute(jnp.transpose(w_out), YX + H, column_moves())

    line = jnp.concatenate(
        [
            jnp.concatenate([columns[:, :256], by_part[0], by_part[1], by_part[2]], axis=1),
            jnp.concatenate([columns[:, 128:], got[0], got[1], got[2]], axis=1),
        ],
        axis=0,
    )
    line, rows = lax.optimization_barrier((line, rows))
    weights = lax.all_gather(line, Z, axis=0)

    scales = jnp.transpose(power_two(scale_exp), (1, 2, 0, 3)).reshape(2, 64, 6).astype(jnp.bfloat16)
    scales = jnp.pad(scales, ((0, 0), (0, 0), (0, 384 - 6)))
    text = jnp.transpose(text_kv, (1, 0, 2, 3)).reshape(2, 16, 384)
    package = jnp.concatenate([text, scales], axis=1)
    own_package = jnp.where(first, package[0], package[1])
    far_package = lax.ppermute(jnp.where(first, package[1], package[0]), "xi", swap)
    rows = lax.all_gather(rows, H, axis=0)
    rows, far_package = lax.optimization_barrier((rows, far_package))
    normed = call(norm_kernel, shape(4, 128, 768), (rows, yh.reshape(1)), scalars=(1,))
    normed = lax.all_to_all(normed, X, 0, 0, tiled=True)
    columns = pl.pallas_call(
        column_kernel,
        out_shape=shape(8, 48, 384),
        grid=(1,),
        in_specs=[pl.BlockSpec((8, 96, 2 * HD), lambda step: (0, 0, 0))],
        out_specs=pl.BlockSpec((8, 48, 384), lambda step: (0, 0, 0)),
        compiler_params=pltpu.CompilerParams(vmem_limit_bytes=WIDE_BYTES),
    )(weights)
    normed, columns = lax.optimization_barrier((normed, columns))
    columns = lax.all_gather(columns.reshape(384, 384), YX, axis=0, tiled=True)
    partial = call(
        project_kernel,
        shape(4, 128, 1152),
        (normed, weights),
        scratch=[
            pltpu.VMEM((3, 8, 96, 384), jnp.bfloat16),
            pltpu.SemaphoreType.DMA((3,)),
        ],
        far=(1,),
        flops=2 * 512 * 768 * 1152,
    )
    partial = lax.all_to_all(partial, X, 0, 0, tiled=True)

    own_prev = lax.dynamic_index_in_dim(prev_kv, xi, 1, False)
    start = (32 * yh + 16 * xj + z) * 64
    earlier = jnp.concatenate(
        [
            lax.dynamic_slice_in_dim(own_prev, start, 64, 1),
            lax.dynamic_slice_in_dim(own_prev, start + 512, 64, 1),
        ],
        axis=1,
    )
    queries = call(query_kernel, shape(128, 384), (partial, q_gain.reshape(1, HD)))
    kv_pair = call(
        restore_kernel,
        shape(288, 384),
        (partial, earlier, own_package, far_package, k_gain.reshape(1, HD), image_at),
        scalars=(5,),
    )
    kv_pair = jnp.stack([kv_pair, lax.ppermute(kv_pair, "zi", swap)])
    far_queries = [
        lax.ppermute(queries, "zo", [(i, (i + k) % 4) for i in range(4)]) for k in (2, 1, 3)
    ]
    kv_pair = lax.all_to_all(
        jnp.broadcast_to(kv_pair, (4, 2, 288, 384)), ("yh", "xj"), 0, 0, tiled=True
    ).reshape(8, 288, 384)
    mixed = []
    for k, block in enumerate((*far_queries, queries)):
        part = call(attend_kernel, shape(144, 384), (block, kv_pair), flops=4 * 128 * 1152 * 384)
        if k < 3:
            part = lax.ppermute(part, "zo", [(i, (i - (2, 1, 3)[k]) % 4) for i in range(4)])
        mixed.append(part)
    own, far = call(combine_kernel, (shape(64, 384),) * 2, (*mixed, image_at), scalars=(4,))
    far = lax.ppermute(far, "xi", swap)
    attended = jnp.where(first, jnp.concatenate([own, far]), jnp.concatenate([far, own]))
    attended = lax.all_gather(attended, H, axis=0)
    return call(
        output_kernel,
        shape(2, 64, 768),
        (attended, columns.reshape(4, 2, 8, 48, 384), gates),
        flops=2 * 128 * 1536 * 768,
    )


def solution(mesh):
    names = ("yh", "xj", "xi", "zo", "zi", "yl", "c")
    fine = Mesh(mesh.devices.reshape(2, 2, 2, 4, 2, 2, 2), names)
    patch, head = YX + Z, H
    placed = (
        P(None, patch, head),
        P(None, None, patch, head),
        P(None, None, None, head),
        P(None, None, patch, head),
        P(patch, None, head),
        P(head, patch),
        P(None, None, head),
        P(),
        P(),
        P(),
    )
    return jax.shard_map(
        per_device, mesh=fine, in_specs=placed, out_specs=P(None, patch, head), check_vma=False
    )
```

```python
import jax
import jax.numpy as jnp
from jax import lax
from jax.experimental import pallas as pl
from jax.experimental.pallas import tpu as pltpu
from jax.sharding import Mesh, PartitionSpec as P

HD = 128
EPSILON = 1e-06
CODE_LIMIT = 448.0
LOG2E = 1.4426950408889634
VMEM_BYTES = 16 * 1024 * 1024
WIDE_BYTES = 58 * 1024 * 1024

X = ("xj", "xi")
YX = ("yh",) + X
Z = ("zo", "zi")
H = ("yl", "c")


def call(kernel, out_shapes, operands, scratch=(), scalars=(), far=(), flops=0, limit=VMEM_BYTES):
    return pl.pallas_call(
        kernel,
        out_shape=out_shapes,
        in_specs=[
            pl.BlockSpec(
                memory_space=pltpu.SMEM if at in scalars else pltpu.HBM if at in far else pltpu.VMEM
            )
            for at in range(len(operands))
        ],
        out_specs=jax.tree.map(lambda _: pl.BlockSpec(memory_space=pltpu.VMEM), out_shapes),
        scratch_shapes=scratch,
        compiler_params=pltpu.CompilerParams(vmem_limit_bytes=limit),
        cost_estimate=pl.CostEstimate(flops=flops, bytes_accessed=0, transcendentals=0),
    )(*operands)


def pack_kernel(hidden_ref, table_ref, steps_ref, rows_ref, gate_ref):
    rows_ref[0:128, :] = hidden_ref[...]
    plan = table_ref.shape[1]
    point = lax.broadcasted_iota(jnp.int32, (plan, 768), 0)
    row = lax.broadcasted_iota(jnp.int32, (16, 768), 0)
    modulation = jnp.zeros((16, 768), jnp.float32)
    gates = jnp.zeros((16, 768), jnp.float32)
    for image in range(2):
        chosen = point == steps_ref[image]
        for part in range(3):
            line = jnp.sum(
                jnp.where(chosen, table_ref[part].astype(jnp.float32), 0.0), axis=0, keepdims=True
            )
            if part < 2:
                modulation = jnp.where(row == 2 * image + part, line, modulation)
            else:
                gates = jnp.where(row == image, line, gates)
    rows_ref[128:144, :] = modulation.astype(jnp.bfloat16)
    gate_ref[...] = gates


def norm_kernel(rows_ref, y_ref, out_ref):
    features = 4 * 768
    lower = y_ref[0] == 0
    modulation = rows_ref[:, 128:144, :].astype(jnp.float32)
    for image in range(2):
        shift = modulation[:, 2 * image : 2 * image + 1]
        scale = 1.0 + modulation[:, 2 * image + 1 : 2 * image + 2]
        for start in range(0, 64, 16):
            at = image * 64 + start
            hidden = rows_ref[:, at : at + 16, :].astype(jnp.float32)
            centre = jnp.sum(jnp.sum(hidden, axis=0), axis=-1, keepdims=True) / features
            off = hidden - centre[None]
            variance = jnp.sum(jnp.sum(off * off, axis=0), axis=-1, keepdims=True) / features
            normed = (off * lax.rsqrt(variance + EPSILON)[None] * scale + shift).astype(jnp.bfloat16)
            for x in range(4):
                lanes = slice((x % 2) * 384, (x % 2) * 384 + 384)
                low, high = normed[x // 2][:, lanes], normed[2 + x // 2][:, lanes]
                out_ref[x, at : at + 16, 0:384] = jnp.where(lower, low, high)
                out_ref[x, at : at + 16, 384:768] = jnp.where(lower, high, low)


def column_kernel(weights_ref, columns_ref):
    columns_ref[:, :, 0:256] = weights_ref[:, 0:48, :]
    columns_ref[:, :, 256:384] = weights_ref[:, 48:96, 128:256]


def project_kernel(rows_ref, weights_ref, out_ref, held_ref, arrived):
    copies = [
        pltpu.make_async_copy(
            weights_ref.at[:, :, pl.ds(256 + part * 384, 384)], held_ref.at[part], arrived.at[part]
        )
        for part in range(3)
    ]
    for copy in copies:
        copy.start()
    for part in range(3):
        lanes = slice(part * 384, part * 384 + 384)
        copies[part].wait()
        sums = jnp.zeros((512, 384), jnp.float32)
        for y in range(2):
            sums = sums + jnp.dot(
                rows_ref[:, :, y * 384 : y * 384 + 384].reshape(512, 384),
                held_ref[part, :, y * 48 : y * 48 + 48, :].reshape(384, 384),
                preferred_element_type=jnp.float32,
            )
        for x in range(4):
            for image in range(2):
                at = x * 128 + image * 64
                place = (x % 2) * 64
                out_ref[(x // 2) * 2 + image, place : place + 64, lanes] = sums[
                    at : at + 64
                ].astype(jnp.bfloat16)


def rms_scale(vectors, gain):
    return vectors * lax.rsqrt(jnp.mean(vectors * vectors, axis=-1, keepdims=True) + EPSILON) * gain


def summed(part_ref, at):
    acc = part_ref[0, :, at : at + HD].astype(jnp.float32)
    for source in range(1, 4):
        acc = acc + part_ref[source, :, at : at + HD].astype(jnp.float32)
    return acc


def query_kernel(part_ref, q_gain_ref, q_ref):
    for head in range(3):
        lanes = slice(head * HD, head * HD + HD)
        q_ref[:, lanes] = rms_scale(summed(part_ref, head * HD), q_gain_ref[...]).astype(
            jnp.bfloat16
        )


def restore_kernel(part_ref, prev_ref, kept_ref, got_ref, k_gain_ref, image_ref, kv_ref):
    first = image_ref[0] == 0
    kept, got = (ref[16:80, 0:HD].astype(jnp.float32) for ref in (kept_ref, got_ref))
    scales = jnp.concatenate([jnp.where(first, kept, got), jnp.where(first, got, kept)], axis=0)

    def restored(fresh, kind, head):
        earlier = prev_ref[kind, :, head * HD : head * HD + HD].astype(jnp.float32)
        lane = kind * 3 + head
        scale = scales[:, lane : lane + 1]
        limit = CODE_LIMIT * scale
        scaled = jnp.clip(fresh - earlier, -limit, limit).astype(jnp.bfloat16).astype(jnp.float32)
        return (earlier + scaled).astype(jnp.bfloat16)

    for head in range(3):
        lanes = slice(head * HD, head * HD + HD)
        keys = rms_scale(summed(part_ref, 384 + head * HD), k_gain_ref[...])
        kv_ref[0:128, lanes] = restored(keys, 0, head)
        kv_ref[144:272, lanes] = restored(summed(part_ref, 768 + head * HD), 1, head)
    own, far = (ref[0:16, :].astype(jnp.float32) for ref in (kept_ref, got_ref))
    for kind in range(2):
        text = jnp.concatenate([own[8 * kind : 8 * kind + 8], far[8 * kind : 8 * kind + 8]], axis=0)
        kv_ref[128 + 144 * kind : 144 + 144 * kind, :] = text.astype(jnp.bfloat16)


def split_three(value):
    first = value.astype(jnp.bfloat16)
    rest = value - first.astype(jnp.float32)
    second = rest.astype(jnp.bfloat16)
    third = (rest - second.astype(jnp.float32)).astype(jnp.bfloat16)
    return first, second, third


def attend_kernel(q_ref, kv_ref, o_ref):
    factor = LOG2E * HD**-0.5
    lane = lax.broadcasted_iota(jnp.int32, (128, HD), 1)
    stat = jnp.zeros((128, HD), jnp.float32)
    for head in range(3):
        lanes = slice(head * HD, head * HD + HD)
        keys = kv_ref[:, 0:144, lanes].reshape(1152, HD)
        values = kv_ref[:, 144:288, lanes].reshape(1152, HD)
        logits = lax.dot_general(
            q_ref[:, lanes], keys, (((1,), (1,)), ((), ())), preferred_element_type=jnp.float32
        )
        peak = jnp.max(logits, axis=-1, keepdims=True)
        terms = jnp.exp2((logits - peak) * factor)
        total = jnp.sum(terms, axis=-1, keepdims=True)
        mixed = jnp.dot(terms.astype(jnp.bfloat16), values, preferred_element_type=jnp.float32)
        o_ref[0:128, lanes] = (mixed / total).astype(jnp.bfloat16)
        for place, part in enumerate(split_three(peak * factor + jnp.log2(total))):
            stat = jnp.where(lane == head * 3 + place, part.astype(jnp.float32), stat)
    o_ref[128:144, 0:HD] = stat.T[0:16].astype(jnp.bfloat16)
    o_ref[128:144, HD:384] = jnp.zeros((16, 2 * HD), jnp.bfloat16)


def combine_kernel(p0_ref, p1_ref, p2_ref, p3_ref, image_ref, kept_ref, sent_ref):
    parts = (p0_ref, p1_ref, p2_ref, p3_ref)
    first = image_ref[0] == 0
    blank = jnp.zeros((112, HD), jnp.float32)
    stats = [
        jnp.concatenate([ref[128:144, 0:HD].astype(jnp.float32), blank], axis=0).T for ref in parts
    ]
    for head in range(3):
        lanes = slice(head * HD, head * HD + HD)
        sizes = [
            stat[:, head * 3 : head * 3 + 1]
            + stat[:, head * 3 + 1 : head * 3 + 2]
            + stat[:, head * 3 + 2 : head * 3 + 3]
            for stat in stats
        ]
        top = jnp.maximum(jnp.maximum(sizes[0], sizes[1]), jnp.maximum(sizes[2], sizes[3]))
        shares = [jnp.exp2(size - top) for size in sizes]
        whole = shares[0] + shares[1] + shares[2] + shares[3]
        mixed = shares[0] * parts[0][0:128, lanes].astype(jnp.float32)
        for share, ref in zip(shares[1:], parts[1:]):
            mixed = mixed + share * ref[0:128, lanes].astype(jnp.float32)
        mixed = (mixed / whole).astype(jnp.bfloat16)
        kept_ref[:, lanes] = jnp.where(first, mixed[:64], mixed[64:])
        sent_ref[:, lanes] = jnp.where(first, mixed[64:], mixed[:64])


def output_kernel(attended_ref, weights_ref, gate_ref, out_ref):
    for half in range(2):
        lanes = slice(half * 384, half * 384 + 384)
        sums = jnp.zeros((128, 384), jnp.float32)
        for group in range(4):
            sums = sums + lax.dot_general(
                attended_ref[group],
                weights_ref[group, half].reshape(384, 384),
                (((1,), (1,)), ((), ())),
                preferred_element_type=jnp.float32,
            )
        for image in range(2):
            rows = gate_ref[image : image + 1, lanes] * sums[64 * image : 64 * image + 64]
            out_ref[image, :, lanes] = rows.astype(jnp.bfloat16)


def power_two(exponents):
    summed = jnp.zeros(exponents.shape, jnp.float32)
    for exponent in range(-8, 1):
        summed = summed + jnp.where(exponents == exponent, jnp.float32(2.0**exponent), 0.0)
    return summed


def shape(*dims):
    return jax.ShapeDtypeStruct(dims, jnp.bfloat16)


def column_moves():
    moves = []
    for yh in range(2):
        for x in range(4):
            for yl in range(2):
                for c in range(2):
                    there = ((yl * 4 + 2 * c + x % 2) * 2 + yh) * 2 + x // 2
                    moves.append((((yh * 4 + x) * 2 + yl) * 2 + c, there))
    return moves


def per_device(
    image_hidden, text_kv, prev_kv, scale_exp, w_qkv, w_out, mod_table, timesteps, q_gain, k_gain
):
    yh, xj, xi = (lax.axis_index(name) for name in YX)
    z = lax.axis_index(Z)
    first = xi == 0
    image_at = xi.reshape(1)
    swap = [(0, 1), (1, 0)]
    by_part = jnp.transpose(w_qkv, (1, 0, 2))
    got = lax.ppermute(by_part, "yh", swap)

    rows, gates = call(
        pack_kernel,
        (shape(144, 768), jax.ShapeDtypeStruct((16, 768), jnp.float32)),
        (image_hidden.reshape(128, 768), jnp.transpose(mod_table, (1, 0, 2)), timesteps),
        scalars=(2,),
        limit=WIDE_BYTES,
    )

    columns = lax.ppermute(jnp.transpose(w_out), YX + H, column_moves())

    line = jnp.concatenate(
        [
            jnp.concatenate([columns[:, :256], by_part[0], by_part[1], by_part[2]], axis=1),
            jnp.concatenate([columns[:, 128:], got[0], got[1], got[2]], axis=1),
        ],
        axis=0,
    )
    line, rows = lax.optimization_barrier((line, rows))
    weights = lax.all_gather(line, Z, axis=0)

    scales = jnp.transpose(power_two(scale_exp), (1, 2, 0, 3)).reshape(2, 64, 6).astype(jnp.bfloat16)
    scales = jnp.pad(scales, ((0, 0), (0, 0), (0, 384 - 6)))
    text = jnp.transpose(text_kv, (1, 0, 2, 3)).reshape(2, 16, 384)
    package = jnp.concatenate([text, scales], axis=1)
    own_package = jnp.where(first, package[0], package[1])
    far_package = lax.ppermute(jnp.where(first, package[1], package[0]), "xi", swap)
    rows = lax.all_gather(rows, H, axis=0)
    rows, far_package = lax.optimization_barrier((rows, far_package))
    normed = call(norm_kernel, shape(4, 128, 768), (rows, yh.reshape(1)), scalars=(1,))
    normed = lax.all_to_all(normed, X, 0, 0, tiled=True)
    columns = pl.pallas_call(
        column_kernel,
        out_shape=shape(8, 48, 384),
        grid=(1,),
        in_specs=[pl.BlockSpec((8, 96, 2 * HD), lambda step: (0, 0, 0))],
        out_specs=pl.BlockSpec((8, 48, 384), lambda step: (0, 0, 0)),
        compiler_params=pltpu.CompilerParams(vmem_limit_bytes=WIDE_BYTES),
    )(weights)
    normed, columns = lax.optimization_barrier((normed, columns))
    columns = lax.all_gather(columns.reshape(384, 384), YX, axis=0, tiled=True)
    partial = call(
        project_kernel,
        shape(4, 128, 1152),
        (normed, weights),
        scratch=[
            pltpu.VMEM((3, 8, 96, 384), jnp.bfloat16),
            pltpu.SemaphoreType.DMA((3,)),
        ],
        far=(1,),
        flops=2 * 512 * 768 * 1152,
    )
    partial = lax.all_to_all(partial, X, 0, 0, tiled=True)

    own_prev = lax.dynamic_index_in_dim(prev_kv, xi, 1, False)
    start = (32 * yh + 16 * xj + z) * 64
    earlier = jnp.concatenate(
        [
            lax.dynamic_slice_in_dim(own_prev, start, 64, 1),
            lax.dynamic_slice_in_dim(own_prev, start + 512, 64, 1),
        ],
        axis=1,
    )
    queries = call(query_kernel, shape(128, 384), (partial, q_gain.reshape(1, HD)))
    kv_pair = call(
        restore_kernel,
        shape(288, 384),
        (partial, earlier, own_package, far_package, k_gain.reshape(1, HD), image_at),
        scalars=(5,),
    )
    kv_pair = jnp.stack([kv_pair, lax.ppermute(kv_pair, "zi", swap)])
    far_queries = [
        lax.ppermute(queries, "zo", [(i, (i + k) % 4) for i in range(4)]) for k in (2, 1, 3)
    ]
    kv_pair = lax.all_to_all(
        jnp.broadcast_to(kv_pair, (4, 2, 288, 384)), ("yh", "xj"), 0, 0, tiled=True
    ).reshape(8, 288, 384)
    mixed = []
    for k, block in enumerate((*far_queries, queries)):
        part = call(attend_kernel, shape(144, 384), (block, kv_pair), flops=4 * 128 * 1152 * 384)
        if k < 3:
            part = lax.ppermute(part, "zo", [(i, (i - (2, 1, 3)[k]) % 4) for i in range(4)])
        mixed.append(part)
    own, far = call(combine_kernel, (shape(64, 384),) * 2, (*mixed, image_at), scalars=(4,))
    far = lax.ppermute(far, "xi", swap)
    attended = jnp.where(first, jnp.concatenate([own, far]), jnp.concatenate([far, own]))
    attended = lax.all_gather(attended, H, axis=0)
    return call(
        output_kernel,
        shape(2, 64, 768),
        (attended, columns.reshape(4, 2, 8, 48, 384), gates),
        flops=2 * 128 * 1536 * 768,
    )


def solution(mesh):
    names = ("yh", "xj", "xi", "zo", "zi", "yl", "c")
    fine = Mesh(mesh.devices.reshape(2, 2, 2, 4, 2, 2, 2), names)
    patch, head = YX + Z, H
    placed = (
        P(None, patch, head),
        P(None, None, patch, head),
        P(None, None, None, head),
        P(None, None, patch, head),
        P(patch, None, head),
        P(head, patch),
        P(None, None, head),
        P(),
        P(),
        P(),
    )
    return jax.shard_map(
        per_device, mesh=fine, in_specs=placed, out_specs=P(None, patch, head), check_vma=False
    )
```

```python
import jax
import jax.numpy as jnp
from jax import lax
from jax.experimental import pallas as pl
from jax.experimental.pallas import tpu as pltpu
from jax.sharding import Mesh, PartitionSpec as P

HD = 128
EPSILON = 1e-06
CODE_LIMIT = 448.0
LOG2E = 1.4426950408889634
VMEM_BYTES = 16 * 1024 * 1024
WIDE_BYTES = 58 * 1024 * 1024

X = ("xj", "xi")
YX = ("yh",) + X
Z = ("zo", "zi")
H = ("yl", "c")


def call(kernel, out_shapes, operands, scratch=(), scalars=(), far=(), flops=0, limit=VMEM_BYTES):
    return pl.pallas_call(
        kernel,
        out_shape=out_shapes,
        in_specs=[
            pl.BlockSpec(
                memory_space=pltpu.SMEM if at in scalars else pltpu.HBM if at in far else pltpu.VMEM
            )
            for at in range(len(operands))
        ],
        out_specs=jax.tree.map(lambda _: pl.BlockSpec(memory_space=pltpu.VMEM), out_shapes),
        scratch_shapes=scratch,
        compiler_params=pltpu.CompilerParams(vmem_limit_bytes=limit),
        cost_estimate=pl.CostEstimate(flops=flops, bytes_accessed=0, transcendentals=0),
    )(*operands)


def pack_kernel(hidden_ref, table_ref, steps_ref, rows_ref, gate_ref):
    rows_ref[0:128, :] = hidden_ref[...]
    plan = table_ref.shape[1]
    point = lax.broadcasted_iota(jnp.int32, (plan, 768), 0)
    row = lax.broadcasted_iota(jnp.int32, (16, 768), 0)
    modulation = jnp.zeros((16, 768), jnp.float32)
    gates = jnp.zeros((16, 768), jnp.float32)
    for image in range(2):
        chosen = point == steps_ref[image]
        for part in range(3):
            line = jnp.sum(
                jnp.where(chosen, table_ref[part].astype(jnp.float32), 0.0), axis=0, keepdims=True
            )
            if part < 2:
                modulation = jnp.where(row == 2 * image + part, line, modulation)
            else:
                gates = jnp.where(row == image, line, gates)
    rows_ref[128:144, :] = modulation.astype(jnp.bfloat16)
    gate_ref[...] = gates


def norm_kernel(rows_ref, y_ref, out_ref):
    features = 4 * 768
    lower = y_ref[0] == 0
    modulation = rows_ref[:, 128:144, :].astype(jnp.float32)
    for image in range(2):
        shift = modulation[:, 2 * image : 2 * image + 1]
        scale = 1.0 + modulation[:, 2 * image + 1 : 2 * image + 2]
        for start in range(0, 64, 16):
            at = image * 64 + start
            hidden = rows_ref[:, at : at + 16, :].astype(jnp.float32)
            centre = jnp.sum(jnp.sum(hidden, axis=0), axis=-1, keepdims=True) / features
            off = hidden - centre[None]
            variance = jnp.sum(jnp.sum(off * off, axis=0), axis=-1, keepdims=True) / features
            normed = (off * lax.rsqrt(variance + EPSILON)[None] * scale + shift).astype(jnp.bfloat16)
            for x in range(4):
                lanes = slice((x % 2) * 384, (x % 2) * 384 + 384)
                low, high = normed[x // 2][:, lanes], normed[2 + x // 2][:, lanes]
                out_ref[x, at : at + 16, 0:384] = jnp.where(lower, low, high)
                out_ref[x, at : at + 16, 384:768] = jnp.where(lower, high, low)


def column_kernel(weights_ref, columns_ref):
    columns_ref[:, :, 0:256] = weights_ref[:, 0:48, :]
    columns_ref[:, :, 256:384] = weights_ref[:, 48:96, 128:256]


def project_kernel(rows_ref, weights_ref, out_ref, held_ref, arrived):
    copies = [
        pltpu.make_async_copy(
            weights_ref.at[:, :, pl.ds(256 + part * 384, 384)], held_ref.at[part], arrived.at[part]
        )
        for part in range(3)
    ]
    for copy in copies:
        copy.start()
    for part in range(3):
        lanes = slice(part * 384, part * 384 + 384)
        copies[part].wait()
        sums = jnp.zeros((512, 384), jnp.float32)
        for y in range(2):
            sums = sums + jnp.dot(
                rows_ref[:, :, y * 384 : y * 384 + 384].reshape(512, 384),
                held_ref[part, :, y * 48 : y * 48 + 48, :].reshape(384, 384),
                preferred_element_type=jnp.float32,
            )
        for x in range(4):
            for image in range(2):
                at = x * 128 + image * 64
                place = (x % 2) * 64
                out_ref[(x // 2) * 2 + image, place : place + 64, lanes] = sums[
                    at : at + 64
                ].astype(jnp.bfloat16)


def rms_scale(vectors, gain):
    return vectors * lax.rsqrt(jnp.mean(vectors * vectors, axis=-1, keepdims=True) + EPSILON) * gain


def summed(part_ref, at):
    acc = part_ref[0, :, at : at + HD].astype(jnp.float32)
    for source in range(1, 4):
        acc = acc + part_ref[source, :, at : at + HD].astype(jnp.float32)
    return acc


def query_kernel(part_ref, q_gain_ref, q_ref):
    for head in range(3):
        lanes = slice(head * HD, head * HD + HD)
        q_ref[:, lanes] = rms_scale(summed(part_ref, head * HD), q_gain_ref[...]).astype(
            jnp.bfloat16
        )


def restore_kernel(part_ref, prev_ref, kept_ref, got_ref, k_gain_ref, image_ref, kv_ref):
    first = image_ref[0] == 0
    kept, got = (ref[16:80, 0:HD].astype(jnp.float32) for ref in (kept_ref, got_ref))
    scales = jnp.concatenate([jnp.where(first, kept, got), jnp.where(first, got, kept)], axis=0)

    def restored(fresh, kind, head):
        earlier = prev_ref[kind, :, head * HD : head * HD + HD].astype(jnp.float32)
        lane = kind * 3 + head
        scale = scales[:, lane : lane + 1]
        limit = CODE_LIMIT * scale
        scaled = jnp.clip(fresh - earlier, -limit, limit).astype(jnp.bfloat16).astype(jnp.float32)
        return (earlier + scaled).astype(jnp.bfloat16)

    for head in range(3):
        lanes = slice(head * HD, head * HD + HD)
        keys = rms_scale(summed(part_ref, 384 + head * HD), k_gain_ref[...])
        kv_ref[0:128, lanes] = restored(keys, 0, head)
        kv_ref[144:272, lanes] = restored(summed(part_ref, 768 + head * HD), 1, head)
    own, far = (ref[0:16, :].astype(jnp.float32) for ref in (kept_ref, got_ref))
    for kind in range(2):
        text = jnp.concatenate([own[8 * kind : 8 * kind + 8], far[8 * kind : 8 * kind + 8]], axis=0)
        kv_ref[128 + 144 * kind : 144 + 144 * kind, :] = text.astype(jnp.bfloat16)


def split_three(value):
    first = value.astype(jnp.bfloat16)
    rest = value - first.astype(jnp.float32)
    second = rest.astype(jnp.bfloat16)
    third = (rest - second.astype(jnp.float32)).astype(jnp.bfloat16)
    return first, second, third


def attend_kernel(q_ref, kv_ref, o_ref):
    factor = LOG2E * HD**-0.5
    lane = lax.broadcasted_iota(jnp.int32, (128, HD), 1)
    stat = jnp.zeros((128, HD), jnp.float32)
    for head in range(3):
        lanes = slice(head * HD, head * HD + HD)
        keys = kv_ref[:, 0:144, lanes].reshape(1152, HD)
        values = kv_ref[:, 144:288, lanes].reshape(1152, HD)
        logits = lax.dot_general(
            q_ref[:, lanes], keys, (((1,), (1,)), ((), ())), preferred_element_type=jnp.float32
        )
        peak = jnp.max(logits, axis=-1, keepdims=True)
        terms = jnp.exp2((logits - peak) * factor)
        total = jnp.sum(terms, axis=-1, keepdims=True)
        mixed = jnp.dot(terms.astype(jnp.bfloat16), values, preferred_element_type=jnp.float32)
        o_ref[0:128, lanes] = (mixed / total).astype(jnp.bfloat16)
        for place, part in enumerate(split_three(peak * factor + jnp.log2(total))):
            stat = jnp.where(lane == head * 3 + place, part.astype(jnp.float32), stat)
    o_ref[128:144, 0:HD] = stat.T[0:16].astype(jnp.bfloat16)
    o_ref[128:144, HD:384] = jnp.zeros((16, 2 * HD), jnp.bfloat16)


def combine_kernel(p0_ref, p1_ref, p2_ref, p3_ref, image_ref, kept_ref, sent_ref):
    parts = (p0_ref, p1_ref, p2_ref, p3_ref)
    first = image_ref[0] == 0
    blank = jnp.zeros((112, HD), jnp.float32)
    stats = [
        jnp.concatenate([ref[128:144, 0:HD].astype(jnp.float32), blank], axis=0).T for ref in parts
    ]
    for head in range(3):
        lanes = slice(head * HD, head * HD + HD)
        sizes = [
            stat[:, head * 3 : head * 3 + 1]
            + stat[:, head * 3 + 1 : head * 3 + 2]
            + stat[:, head * 3 + 2 : head * 3 + 3]
            for stat in stats
        ]
        top = jnp.maximum(jnp.maximum(sizes[0], sizes[1]), jnp.maximum(sizes[2], sizes[3]))
        shares = [jnp.exp2(size - top) for size in sizes]
        whole = shares[0] + shares[1] + shares[2] + shares[3]
        mixed = shares[0] * parts[0][0:128, lanes].astype(jnp.float32)
        for share, ref in zip(shares[1:], parts[1:]):
            mixed = mixed + share * ref[0:128, lanes].astype(jnp.float32)
        mixed = (mixed / whole).astype(jnp.bfloat16)
        kept_ref[:, lanes] = jnp.where(first, mixed[:64], mixed[64:])
        sent_ref[:, lanes] = jnp.where(first, mixed[64:], mixed[:64])


def output_kernel(attended_ref, weights_ref, gate_ref, out_ref):
    sums = jnp.zeros((128, 384), jnp.float32)
    for group in range(4):
        sums = sums + lax.dot_general(
            attended_ref[group],
            weights_ref[group].reshape(384, 384),
            (((1,), (1,)), ((), ())),
            preferred_element_type=jnp.float32,
        )
    for image in range(2):
        rows = gate_ref[image : image + 1, :] * sums[64 * image : 64 * image + 64]
        out_ref[image] = rows.astype(jnp.bfloat16)


def power_two(exponents):
    summed = jnp.zeros(exponents.shape, jnp.float32)
    for exponent in range(-8, 1):
        summed = summed + jnp.where(exponents == exponent, jnp.float32(2.0**exponent), 0.0)
    return summed


def shape(*dims):
    return jax.ShapeDtypeStruct(dims, jnp.bfloat16)


def column_moves():
    moves = []
    for yh in range(2):
        for x in range(4):
            for yl in range(2):
                for c in range(2):
                    there = ((yl * 4 + 2 * c + x % 2) * 2 + yh) * 2 + x // 2
                    moves.append((((yh * 4 + x) * 2 + yl) * 2 + c, there))
    return moves


def per_device(
    image_hidden, text_kv, prev_kv, scale_exp, w_qkv, w_out, mod_table, timesteps, q_gain, k_gain
):
    yh, xj, xi = (lax.axis_index(name) for name in YX)
    z = lax.axis_index(Z)
    first = xi == 0
    image_at = xi.reshape(1)
    swap = [(0, 1), (1, 0)]
    by_part = jnp.transpose(w_qkv, (1, 0, 2))
    got = lax.ppermute(by_part, "yh", swap)

    rows, gates = call(
        pack_kernel,
        (shape(144, 768), jax.ShapeDtypeStruct((16, 768), jnp.float32)),
        (image_hidden.reshape(128, 768), jnp.transpose(mod_table, (1, 0, 2)), timesteps),
        scalars=(2,),
        limit=WIDE_BYTES,
    )

    columns = lax.ppermute(jnp.transpose(w_out), YX + H, column_moves())

    line = jnp.concatenate(
        [
            jnp.concatenate([columns[:, :256], by_part[0], by_part[1], by_part[2]], axis=1),
            jnp.concatenate([columns[:, 128:], got[0], got[1], got[2]], axis=1),
        ],
        axis=0,
    )
    line, rows = lax.optimization_barrier((line, rows))
    weights = lax.all_gather(line, Z, axis=0)

    scales = jnp.transpose(power_two(scale_exp), (1, 2, 0, 3)).reshape(2, 64, 6).astype(jnp.bfloat16)
    scales = jnp.pad(scales, ((0, 0), (0, 0), (0, 384 - 6)))
    text = jnp.transpose(text_kv, (1, 0, 2, 3)).reshape(2, 16, 384)
    package = jnp.concatenate([text, scales], axis=1)
    own_package = jnp.where(first, package[0], package[1])
    far_package = lax.ppermute(jnp.where(first, package[1], package[0]), "xi", swap)
    rows = lax.all_gather(rows, H, axis=0)
    rows, far_package = lax.optimization_barrier((rows, far_package))
    normed = call(norm_kernel, shape(4, 128, 768), (rows, yh.reshape(1)), scalars=(1,))
    normed = lax.all_to_all(normed, X, 0, 0, tiled=True)
    columns = pl.pallas_call(
        column_kernel,
        out_shape=shape(8, 48, 384),
        grid=(1,),
        in_specs=[pl.BlockSpec((8, 96, 2 * HD), lambda step: (0, 0, 0))],
        out_specs=pl.BlockSpec((8, 48, 384), lambda step: (0, 0, 0)),
        compiler_params=pltpu.CompilerParams(vmem_limit_bytes=WIDE_BYTES),
    )(weights)
    normed, columns = lax.optimization_barrier((normed, columns))
    columns = lax.all_gather(columns.reshape(384, 384), YX, axis=0, tiled=True)
    partial = call(
        project_kernel,
        shape(4, 128, 1152),
        (normed, weights),
        scratch=[
            pltpu.VMEM((3, 8, 96, 384), jnp.bfloat16),
            pltpu.SemaphoreType.DMA((3,)),
        ],
        far=(1,),
        flops=2 * 512 * 768 * 1152,
    )
    partial = lax.all_to_all(partial, X, 0, 0, tiled=True)

    own_prev = lax.dynamic_index_in_dim(prev_kv, xi, 1, False)
    start = (32 * yh + 16 * xj + z) * 64
    earlier = jnp.concatenate(
        [
            lax.dynamic_slice_in_dim(own_prev, start, 64, 1),
            lax.dynamic_slice_in_dim(own_prev, start + 512, 64, 1),
        ],
        axis=1,
    )
    queries = call(query_kernel, shape(128, 384), (partial, q_gain.reshape(1, HD)))
    kv_pair = call(
        restore_kernel,
        shape(288, 384),
        (partial, earlier, own_package, far_package, k_gain.reshape(1, HD), image_at),
        scalars=(5,),
    )
    kv_pair = jnp.stack([kv_pair, lax.ppermute(kv_pair, "zi", swap)])
    far_queries = [
        lax.ppermute(queries, "zo", [(i, (i + k) % 4) for i in range(4)]) for k in (2, 1, 3)
    ]
    kv_pair = lax.all_to_all(
        jnp.broadcast_to(kv_pair, (4, 2, 288, 384)), ("xj", "yh"), 0, 0, tiled=True
    ).reshape(8, 288, 384)
    mixed = []
    for k, block in enumerate((*far_queries, queries)):
        part = call(attend_kernel, shape(144, 384), (block, kv_pair), flops=4 * 128 * 1152 * 384)
        if k < 3:
            part = lax.ppermute(part, "zo", [(i, (i - (2, 1, 3)[k]) % 4) for i in range(4)])
        mixed.append(part)
    own, far = call(combine_kernel, (shape(64, 384),) * 2, (*mixed, image_at), scalars=(4,))
    far = lax.ppermute(far, "xi", swap)
    attended = jnp.where(first, jnp.concatenate([own, far]), jnp.concatenate([far, own]))
    attended = lax.all_gather(attended, H, axis=0)
    return pl.pallas_call(
        output_kernel,
        out_shape=shape(2, 64, 768),
        grid=(2,),
        in_specs=[
            pl.BlockSpec((4, 128, 384), lambda half: (0, 0, 0)),
            pl.BlockSpec((4, None, 8, 48, 384), lambda half: (0, half, 0, 0, 0)),
            pl.BlockSpec((16, 384), lambda half: (0, half)),
        ],
        out_specs=pl.BlockSpec((2, 64, 384), lambda half: (0, 0, half)),
        compiler_params=pltpu.CompilerParams(vmem_limit_bytes=WIDE_BYTES),
        cost_estimate=pl.CostEstimate(
            flops=2 * 128 * 1536 * 768, bytes_accessed=0, transcendentals=0
        ),
    )(attended, columns.reshape(4, 2, 8, 48, 384), gates)


def solution(mesh):
    names = ("yh", "xj", "xi", "zo", "zi", "yl", "c")
    fine = Mesh(mesh.devices.reshape(2, 2, 2, 4, 2, 2, 2), names)
    patch, head = YX + Z, H
    placed = (
        P(None, patch, head),
        P(None, None, patch, head),
        P(None, None, None, head),
        P(None, None, patch, head),
        P(patch, None, head),
        P(head, patch),
        P(None, None, head),
        P(),
        P(),
        P(),
    )
    return jax.shard_map(
        per_device, mesh=fine, in_specs=placed, out_specs=P(None, patch, head), check_vma=False
    )
```

```python
import jax
import jax.numpy as jnp
from jax import lax
from jax.experimental import pallas as pl
from jax.experimental.pallas import tpu as pltpu
from jax.sharding import Mesh, PartitionSpec as P

HD = 128
EPSILON = 1e-06
CODE_LIMIT = 448.0
LOG2E = 1.4426950408889634
VMEM_BYTES = 16 * 1024 * 1024
WIDE_BYTES = 58 * 1024 * 1024

X = ("xj", "xi")
YX = ("yh",) + X
Z = ("zo", "zi")
H = ("yl", "c")


def call(kernel, out_shapes, operands, scratch=(), scalars=(), far=(), flops=0, limit=VMEM_BYTES):
    return pl.pallas_call(
        kernel,
        out_shape=out_shapes,
        in_specs=[
            pl.BlockSpec(
                memory_space=pltpu.SMEM if at in scalars else pltpu.HBM if at in far else pltpu.VMEM
            )
            for at in range(len(operands))
        ],
        out_specs=jax.tree.map(lambda _: pl.BlockSpec(memory_space=pltpu.VMEM), out_shapes),
        scratch_shapes=scratch,
        compiler_params=pltpu.CompilerParams(vmem_limit_bytes=limit),
        cost_estimate=pl.CostEstimate(flops=flops, bytes_accessed=0, transcendentals=0),
    )(*operands)


def pack_kernel(hidden_ref, table_ref, steps_ref, rows_ref, gate_ref):
    rows_ref[0:128, :] = hidden_ref[...]
    plan = table_ref.shape[1]
    point = lax.broadcasted_iota(jnp.int32, (plan, 768), 0)
    row = lax.broadcasted_iota(jnp.int32, (16, 768), 0)
    modulation = jnp.zeros((16, 768), jnp.float32)
    gates = jnp.zeros((16, 768), jnp.float32)
    for image in range(2):
        chosen = point == steps_ref[image]
        for part in range(3):
            line = jnp.sum(
                jnp.where(chosen, table_ref[part].astype(jnp.float32), 0.0), axis=0, keepdims=True
            )
            if part < 2:
                modulation = jnp.where(row == 2 * image + part, line, modulation)
            else:
                gates = jnp.where(row == image, line, gates)
    rows_ref[128:144, :] = modulation.astype(jnp.bfloat16)
    gate_ref[...] = gates


def norm_kernel(rows_ref, y_ref, out_ref):
    features = 4 * 768
    lower = y_ref[0] == 0
    modulation = rows_ref[:, 128:144, :].astype(jnp.float32)
    for image in range(2):
        shift = modulation[:, 2 * image : 2 * image + 1]
        scale = 1.0 + modulation[:, 2 * image + 1 : 2 * image + 2]
        for start in range(0, 64, 16):
            at = image * 64 + start
            hidden = rows_ref[:, at : at + 16, :].astype(jnp.float32)
            centre = jnp.sum(jnp.sum(hidden, axis=0), axis=-1, keepdims=True) / features
            off = hidden - centre[None]
            variance = jnp.sum(jnp.sum(off * off, axis=0), axis=-1, keepdims=True) / features
            normed = (off * lax.rsqrt(variance + EPSILON)[None] * scale + shift).astype(jnp.bfloat16)
            for x in range(4):
                lanes = slice((x % 2) * 384, (x % 2) * 384 + 384)
                low, high = normed[x // 2][:, lanes], normed[2 + x // 2][:, lanes]
                out_ref[x, at : at + 16, 0:384] = jnp.where(lower, low, high)
                out_ref[x, at : at + 16, 384:768] = jnp.where(lower, high, low)


def column_kernel(weights_ref, columns_ref):
    columns_ref[:, :, 0:256] = weights_ref[:, 0:48, :]
    columns_ref[:, :, 256:384] = weights_ref[:, 48:96, 128:256]


def project_kernel(rows_ref, weights_ref, out_ref, held_ref, arrived):
    copies = [
        pltpu.make_async_copy(
            weights_ref.at[:, :, pl.ds(256 + part * 384, 384)], held_ref.at[part], arrived.at[part]
        )
        for part in range(3)
    ]
    for copy in copies:
        copy.start()
    for part in range(3):
        lanes = slice(part * 384, part * 384 + 384)
        copies[part].wait()
        sums = jnp.zeros((512, 384), jnp.float32)
        for y in range(2):
            sums = sums + jnp.dot(
                rows_ref[:, :, y * 384 : y * 384 + 384].reshape(512, 384),
                held_ref[part, :, y * 48 : y * 48 + 48, :].reshape(384, 384),
                preferred_element_type=jnp.float32,
            )
        for x in range(4):
            for image in range(2):
                at = x * 128 + image * 64
                place = (x % 2) * 64
                out_ref[(x // 2) * 2 + image, place : place + 64, lanes] = sums[
                    at : at + 64
                ].astype(jnp.bfloat16)


def rms_scale(vectors, gain):
    return vectors * lax.rsqrt(jnp.mean(vectors * vectors, axis=-1, keepdims=True) + EPSILON) * gain


def summed(part_ref, at):
    acc = part_ref[0, :, at : at + HD].astype(jnp.float32)
    for source in range(1, 4):
        acc = acc + part_ref[source, :, at : at + HD].astype(jnp.float32)
    return acc


def query_kernel(part_ref, q_gain_ref, q_ref):
    for head in range(3):
        lanes = slice(head * HD, head * HD + HD)
        q_ref[:, lanes] = rms_scale(summed(part_ref, head * HD), q_gain_ref[...]).astype(
            jnp.bfloat16
        )


def restore_kernel(part_ref, prev_ref, kept_ref, got_ref, k_gain_ref, image_ref, kv_ref):
    first = image_ref[0] == 0
    kept, got = (ref[16:80, 0:HD].astype(jnp.float32) for ref in (kept_ref, got_ref))
    scales = jnp.concatenate([jnp.where(first, kept, got), jnp.where(first, got, kept)], axis=0)

    def restored(fresh, kind, head):
        earlier = prev_ref[kind, :, head * HD : head * HD + HD].astype(jnp.float32)
        lane = kind * 3 + head
        scale = scales[:, lane : lane + 1]
        limit = CODE_LIMIT * scale
        scaled = jnp.clip(fresh - earlier, -limit, limit).astype(jnp.bfloat16).astype(jnp.float32)
        return (earlier + scaled).astype(jnp.bfloat16)

    for head in range(3):
        lanes = slice(head * HD, head * HD + HD)
        keys = rms_scale(summed(part_ref, 384 + head * HD), k_gain_ref[...])
        kv_ref[0:128, lanes] = restored(keys, 0, head)
        kv_ref[144:272, lanes] = restored(summed(part_ref, 768 + head * HD), 1, head)
    own, far = (ref[0:16, :].astype(jnp.float32) for ref in (kept_ref, got_ref))
    for kind in range(2):
        text = jnp.concatenate([own[8 * kind : 8 * kind + 8], far[8 * kind : 8 * kind + 8]], axis=0)
        kv_ref[128 + 144 * kind : 144 + 144 * kind, :] = text.astype(jnp.bfloat16)


def split_three(value):
    first = value.astype(jnp.bfloat16)
    rest = value - first.astype(jnp.float32)
    second = rest.astype(jnp.bfloat16)
    third = (rest - second.astype(jnp.float32)).astype(jnp.bfloat16)
    return first, second, third


def attend_kernel(q_ref, kv_ref, o_ref):
    factor = LOG2E * HD**-0.5
    lane = lax.broadcasted_iota(jnp.int32, (128, HD), 1)
    stat = jnp.zeros((128, HD), jnp.float32)
    for head in range(3):
        lanes = slice(head * HD, head * HD + HD)
        keys = kv_ref[:, 0:144, lanes].reshape(1152, HD)
        values = kv_ref[:, 144:288, lanes].reshape(1152, HD)
        logits = lax.dot_general(
            q_ref[:, lanes], keys, (((1,), (1,)), ((), ())), preferred_element_type=jnp.float32
        )
        peak = jnp.max(logits, axis=-1, keepdims=True)
        terms = jnp.exp2((logits - peak) * factor)
        total = jnp.sum(terms, axis=-1, keepdims=True)
        mixed = jnp.dot(terms.astype(jnp.bfloat16), values, preferred_element_type=jnp.float32)
        o_ref[0:128, lanes] = (mixed / total).astype(jnp.bfloat16)
        for place, part in enumerate(split_three(peak * factor + jnp.log2(total))):
            stat = jnp.where(lane == head * 3 + place, part.astype(jnp.float32), stat)
    o_ref[128:144, 0:HD] = stat.T[0:16].astype(jnp.bfloat16)
    o_ref[128:144, HD:384] = jnp.zeros((16, 2 * HD), jnp.bfloat16)


def combine_kernel(p0_ref, p1_ref, p2_ref, p3_ref, image_ref, kept_ref, sent_ref):
    parts = (p0_ref, p1_ref, p2_ref, p3_ref)
    first = image_ref[0] == 0
    blank = jnp.zeros((112, HD), jnp.float32)
    stats = [
        jnp.concatenate([ref[128:144, 0:HD].astype(jnp.float32), blank], axis=0).T for ref in parts
    ]
    for head in range(3):
        lanes = slice(head * HD, head * HD + HD)
        sizes = [
            stat[:, head * 3 : head * 3 + 1]
            + stat[:, head * 3 + 1 : head * 3 + 2]
            + stat[:, head * 3 + 2 : head * 3 + 3]
            for stat in stats
        ]
        top = jnp.maximum(jnp.maximum(sizes[0], sizes[1]), jnp.maximum(sizes[2], sizes[3]))
        shares = [jnp.exp2(size - top) for size in sizes]
        whole = shares[0] + shares[1] + shares[2] + shares[3]
        mixed = shares[0] * parts[0][0:128, lanes].astype(jnp.float32)
        for share, ref in zip(shares[1:], parts[1:]):
            mixed = mixed + share * ref[0:128, lanes].astype(jnp.float32)
        mixed = (mixed / whole).astype(jnp.bfloat16)
        kept_ref[:, lanes] = jnp.where(first, mixed[:64], mixed[64:])
        sent_ref[:, lanes] = jnp.where(first, mixed[64:], mixed[:64])


def output_kernel(attended_ref, weights_ref, gate_ref, out_ref):
    for half in range(2):
        lanes = slice(half * 384, half * 384 + 384)
        sums = jnp.zeros((128, 384), jnp.float32)
        for group in range(4):
            sums = sums + lax.dot_general(
                attended_ref[group],
                weights_ref[group, half].reshape(384, 384),
                (((1,), (1,)), ((), ())),
                preferred_element_type=jnp.float32,
            )
        for image in range(2):
            rows = gate_ref[image : image + 1, lanes] * sums[64 * image : 64 * image + 64]
            out_ref[image, :, lanes] = rows.astype(jnp.bfloat16)


def power_two(exponents):
    summed = jnp.zeros(exponents.shape, jnp.float32)
    for exponent in range(-8, 1):
        summed = summed + jnp.where(exponents == exponent, jnp.float32(2.0**exponent), 0.0)
    return summed


def shape(*dims):
    return jax.ShapeDtypeStruct(dims, jnp.bfloat16)


def column_moves():
    moves = []
    for yh in range(2):
        for x in range(4):
            for yl in range(2):
                for c in range(2):
                    there = ((yl * 4 + 2 * c + x % 2) * 2 + yh) * 2 + x // 2
                    moves.append((((yh * 4 + x) * 2 + yl) * 2 + c, there))
    return moves


def per_device(
    image_hidden, text_kv, prev_kv, scale_exp, w_qkv, w_out, mod_table, timesteps, q_gain, k_gain
):
    yh, xj, xi = (lax.axis_index(name) for name in YX)
    z = lax.axis_index(Z)
    first = xi == 0
    image_at = xi.reshape(1)
    swap = [(0, 1), (1, 0)]
    by_part = jnp.transpose(w_qkv, (1, 0, 2))
    got = lax.ppermute(by_part, "yh", swap)

    rows, gates = call(
        pack_kernel,
        (shape(144, 768), jax.ShapeDtypeStruct((16, 768), jnp.float32)),
        (image_hidden.reshape(128, 768), jnp.transpose(mod_table, (1, 0, 2)), timesteps),
        scalars=(2,),
        limit=WIDE_BYTES,
    )

    columns = lax.ppermute(jnp.transpose(w_out), YX + H, column_moves())

    line = jnp.concatenate(
        [
            jnp.concatenate([columns[:, :256], by_part[0], by_part[1], by_part[2]], axis=1),
            jnp.concatenate([columns[:, 128:], got[0], got[1], got[2]], axis=1),
        ],
        axis=0,
    )
    line, rows = lax.optimization_barrier((line, rows))
    weights = lax.all_gather(line, Z, axis=0)

    scales = jnp.transpose(power_two(scale_exp), (1, 2, 0, 3)).reshape(2, 64, 6).astype(jnp.bfloat16)
    scales = jnp.pad(scales, ((0, 0), (0, 0), (0, 384 - 6)))
    text = jnp.transpose(text_kv, (1, 0, 2, 3)).reshape(2, 16, 384)
    package = jnp.concatenate([text, scales], axis=1)
    own_package = jnp.where(first, package[0], package[1])
    far_package = lax.ppermute(jnp.where(first, package[1], package[0]), "xi", swap)
    rows = lax.all_gather(rows, H, axis=0)
    rows, far_package = lax.optimization_barrier((rows, far_package))
    normed = call(norm_kernel, shape(4, 128, 768), (rows, yh.reshape(1)), scalars=(1,))
    normed = lax.all_to_all(normed, X, 0, 0, tiled=True)
    columns = pl.pallas_call(
        column_kernel,
        out_shape=shape(8, 48, 384),
        grid=(1,),
        in_specs=[pl.BlockSpec((8, 96, 2 * HD), lambda step: (0, 0, 0))],
        out_specs=pl.BlockSpec((8, 48, 384), lambda step: (0, 0, 0)),
        compiler_params=pltpu.CompilerParams(vmem_limit_bytes=WIDE_BYTES),
    )(weights)
    normed, columns = lax.optimization_barrier((normed, columns))
    columns = lax.all_gather(columns.reshape(384, 384), YX, axis=0, tiled=True)
    partial = call(
        project_kernel,
        shape(4, 128, 1152),
        (normed, weights),
        scratch=[
            pltpu.VMEM((3, 8, 96, 384), jnp.bfloat16),
            pltpu.SemaphoreType.DMA((3,)),
        ],
        far=(1,),
        flops=2 * 512 * 768 * 1152,
    )
    partial = lax.all_to_all(partial, X, 0, 0, tiled=True)

    own_prev = lax.dynamic_index_in_dim(prev_kv, xi, 1, False)
    start = (32 * yh + 16 * xj + z) * 64
    earlier = jnp.concatenate(
        [
            lax.dynamic_slice_in_dim(own_prev, start, 64, 1),
            lax.dynamic_slice_in_dim(own_prev, start + 512, 64, 1),
        ],
        axis=1,
    )
    queries = call(query_kernel, shape(128, 384), (partial, q_gain.reshape(1, HD)))
    kv_pair = call(
        restore_kernel,
        shape(288, 384),
        (partial, earlier, own_package, far_package, k_gain.reshape(1, HD), image_at),
        scalars=(5,),
    )
    kv_pair = jnp.stack([kv_pair, lax.ppermute(kv_pair, "zi", swap)])
    far_queries = [
        lax.ppermute(queries, "zo", [(i, (i + k) % 4) for i in range(4)]) for k in (2, 1, 3)
    ]
    kv_pair = lax.all_to_all(
        jnp.broadcast_to(kv_pair, (4, 2, 288, 384)), ("xj", "yh"), 0, 0, tiled=True
    ).reshape(8, 288, 384)
    mixed = []
    for k, block in enumerate((*far_queries, queries)):
        part = call(attend_kernel, shape(144, 384), (block, kv_pair), flops=4 * 128 * 1152 * 384)
        if k < 3:
            part = lax.ppermute(part, "zo", [(i, (i - (2, 1, 3)[k]) % 4) for i in range(4)])
        mixed.append(part)
    own, far = call(combine_kernel, (shape(64, 384),) * 2, (*mixed, image_at), scalars=(4,))
    far = lax.ppermute(far, "xi", swap)
    attended = jnp.where(first, jnp.concatenate([own, far]), jnp.concatenate([far, own]))
    attended = lax.all_gather(attended, H, axis=0)
    return call(
        output_kernel,
        shape(2, 64, 768),
        (attended, columns.reshape(4, 2, 8, 48, 384), gates),
        flops=2 * 128 * 1536 * 768,
    )


def solution(mesh):
    names = ("yh", "xj", "xi", "zo", "zi", "yl", "c")
    fine = Mesh(mesh.devices.reshape(2, 2, 2, 4, 2, 2, 2), names)
    patch, head = YX + Z, H
    placed = (
        P(None, patch, head),
        P(None, None, patch, head),
        P(None, None, None, head),
        P(None, None, patch, head),
        P(patch, None, head),
        P(head, patch),
        P(None, None, head),
        P(),
        P(),
        P(),
    )
    return jax.shard_map(
        per_device, mesh=fine, in_specs=placed, out_specs=P(None, patch, head), check_vma=False
    )
```
